128 devices in a mesh: cam: 32 (over z, x, core), trk: 4 (over y).
Axes of the slice: x: 4, y: 4, z: 4, core: 2. Of those that a mesh axis runs over, the one named last changes fastest.
Arguments:
- grad_cam: float32 [128, 768], P('cam'), may hold values from -6 to 6
- cam_diag: float32 [128, 768], P('cam'), may hold values from 4 to 8
- precond: float32 [128, 768], P('cam'), may hold values from 0.12 to 0.3
- point_inv: float32 [2048, 9, 128], P(('cam', 'trk')), may hold values from -0.15 to 1.2, as said below
- tiles: bfloat16 [3072, 768, 384], P(('cam', 'trk')), may hold values from -0.0234375 to 0.0234375
- tile_block: int32 [3072], P(('cam', 'trk')), may hold values from 0 to 3
- tile_owner: int32 [3072], P(('cam', 'trk')), may hold values from 0 to 31, as said below
- tile_track: int32 [3072], P(('cam', 'trk')), may hold values from 0 to 15, as said below
- tile_live: int32 [128], P(('cam', 'trk')), may hold values from 6 to 24, as said below
- covis: bfloat16 [512, 768, 768], P(('cam', 'trk')), may hold values from -0.0546875 to 0.0546875
- pair_row: int32 [512], P(('cam', 'trk')), may hold values from 0 to 3
- pair_col: int32 [512], P(('cam', 'trk')), may hold values from 0 to 127, as said below
Outputs:
- step_field: float32 [128, 768], P('cam')
- residual: float32 [128, 768], P('cam')
The draws below stay inside these ranges and needn't reach their ends.
Inputs may be any that keep to these rules, and one draw needn't show every extreme that they name: `tile_owner`: at most 4 tiles of one device name one owner, and on every device some owner is named by exactly 4 of its live tiles. `tile_track`: no two tiles of one device name the same owner and track tile. `tile_live`: some device has all 24 tiles live. `pair_col`: A pair's two camera blocks differ. `point_inv`: each point's block is symmetric positive definite.
All inputs are finite; a program needn't handle non-finite values.
Results may differ from the reference program's by a relative error of at most 0.0035.
Values may be sent and summed in bfloat16 or wider, within the bound.
A program may use at most 64 MiB of HBM per device.

```python
import math
import jax
import jax.numpy as jnp
from jax import lax

TRKT = 128
CB_DEV = 4
NT_DEV = 24
TT_DEV = 16
NU_DEV = 4
SLOT = 4
ITERS = 2
KB = 768
TQ = 384
NB = 128
NTILES = 3072
NTT = 2048
NPAIR = 512
N_CAM = 32
N_TRK = 4


def route_table(key):
    devices = N_CAM * N_TRK
    device_keys = jax.random.split(key, devices)
    orders = jax.vmap(lambda one_key: jax.random.permutation(one_key, N_CAM))(device_keys)
    offsets = jax.random.randint(jax.random.fold_in(key, 5), (devices, N_CAM), 0, TT_DEV)
    positions = jnp.arange(NT_DEV)
    group_index = jnp.where(positions < SLOT, 0, 1 + (positions - SLOT) % (N_CAM - 1))
    occurrence = jnp.where(positions < SLOT, positions, (positions - SLOT) // (N_CAM - 1))
    owners = orders[:, group_index]
    track_local = (offsets[:, group_index] + occurrence[None, :]) % TT_DEV
    lowest = max(SLOT, NT_DEV // 4)
    head_keys = jax.random.split(jax.random.fold_in(key, 6), devices)
    tail_keys = jax.random.split(jax.random.fold_in(key, 8), devices)
    heads = jax.vmap(lambda one_key: jax.random.permutation(one_key, lowest))(head_keys)
    tails = jax.vmap(lambda one_key: jax.random.permutation(one_key, NT_DEV - lowest))(tail_keys) + lowest
    shuffle = jnp.concatenate([heads, tails], axis=1)
    owners = jnp.take_along_axis(owners, shuffle, axis=1)
    track_local = jnp.take_along_axis(track_local, shuffle, axis=1)
    return (owners.reshape(-1).astype(jnp.int32), track_local.reshape(-1).astype(jnp.int32))


def pair_table(key):
    row_local = jax.random.randint(jax.random.fold_in(key, 21), (NPAIR,), 0, CB_DEV)
    row_global = jnp.arange(NPAIR) // (NU_DEV * N_TRK) * CB_DEV + row_local
    jumps = jax.random.randint(jax.random.fold_in(key, 23), (NPAIR,), 0, NB - 1)
    columns = (row_global + 1 + jumps) % NB
    return (row_local.astype(jnp.int32), columns.astype(jnp.int32))


def draw_tile_owner(key, part):
    return route_table(key)[0]


def draw_tile_track(key, part):
    return route_table(key)[1]


def draw_pair_row(key, part):
    return pair_table(key)[0]


def draw_pair_col(key, part):
    return pair_table(key)[1]


def draw_tile_live(key, part):
    key = jax.random.fold_in(key, 7)
    devices = N_CAM * N_TRK
    lowest = max(SLOT, NT_DEV // 4)
    counts = jax.random.randint(key, (devices,), lowest, NT_DEV + 1)
    chosen = jax.random.randint(jax.random.fold_in(key, 1), (), 0, devices)
    return counts.at[chosen].set(NT_DEV).astype(jnp.int32)


def draw_point_inv(key, part):
    key = jax.random.fold_in(key, 9)
    diagonal = jnp.exp(jax.random.uniform(key, (NTT, 3, TRKT), jnp.float32, jnp.log(0.4), jnp.log(1.2)))
    offdiag = jax.random.uniform(jax.random.fold_in(key, 2), (NTT, 3, TRKT), jnp.float32, -0.15, 0.15)
    entries = [diagonal[:, 0], offdiag[:, 0], offdiag[:, 1], offdiag[:, 0], diagonal[:, 1], offdiag[:, 2], offdiag[:, 1], offdiag[:, 2], diagonal[:, 2]]
    return jnp.stack(entries, axis=1).astype(jnp.float32)


def with_ends(array, stream_key, low, high):
    longest = array.shape.index(max(array.shape))
    spots = []
    for shift in (0, 1):
        where = [jax.random.randint(jax.random.fold_in(stream_key, axis), (), 0, length) for axis, length in enumerate(array.shape)]
        where[longest] = (where[longest] + shift) % array.shape[longest]
        spots.append(tuple(where))
    return array.at[spots[0]].set(low).at[spots[1]].set(high)


def block_scale(rng, shape, cuts, smallest, top_value):
    level, own = 1.0, jax.random.fold_in(rng, 6)
    for position, parts in cuts:
        heights = jnp.exp(jax.random.uniform(jax.random.fold_in(own, position), (parts,), jnp.float32, smallest / len(cuts), top_value / len(cuts)))
        level = level * jnp.repeat(heights, shape[position] // parts).reshape([-1 if axis == position else 1 for axis in range(len(shape))])
    return level


def bell_draw(stream_key, shape, width, reach, shards=(), held_as=jnp.bfloat16):
    result = jax.random.normal(stream_key, shape, jnp.float32) * width
    if len(shards) > 0:
        result = block_scale(stream_key, shape, shards, -0.22, 0.18) * result
    return jnp.clip(result, min=-reach, max=reach).astype(held_as)


def setup_inputs(seed: int = 0) -> dict:
    seeds = jax.random.split(jax.random.key(seed), 13)
    grad_cam = bell_draw(seeds[0], (NB, KB), 1.0, 6.0, ((0, 32),), jnp.float32)
    cam_diag = jnp.clip(4.0 + 4.0 * jax.random.uniform(seeds[1], (NB, KB), jnp.float32) ** block_scale(seeds[1], (NB, KB), ((0, 32),), -0.2, 0.2), 4.0, 8.0)
    precond = jnp.clip(jnp.exp(math.log(0.3) - 0.9162908 * jax.random.uniform(seeds[2], (NB, KB), jnp.float32) ** block_scale(seeds[2], (NB, KB), ((0, 32),), -0.2, 0.2)), 0.12, 0.3)
    point_inv = draw_point_inv(jax.random.fold_in(seeds[12], 71), 0)
    tiles = bell_draw(seeds[4], (NTILES, KB, TQ), (2 * (KB + NT_DEV * N_TRK * TQ)) ** -0.5, 0.0234375, ((0, 128),))
    tile_block = with_ends(jax.random.randint(seeds[5], (NTILES,), 0, CB_DEV), jax.random.fold_in(seeds[5], 1), 0, CB_DEV - 1).astype(jnp.int32)
    tile_owner = draw_tile_owner(jax.random.fold_in(seeds[12], 71), 0)
    tile_track = draw_tile_track(jax.random.fold_in(seeds[12], 71), 0)
    tile_live = draw_tile_live(jax.random.fold_in(seeds[12], 71), 0)
    covis = bell_draw(seeds[9], (NPAIR, KB, KB), (4 * KB * NU_DEV * N_TRK // CB_DEV) ** -0.5, 0.0546875, ((0, 128),))
    pair_row = draw_pair_row(jax.random.fold_in(seeds[12], 71), 0)
    pair_col = draw_pair_col(jax.random.fold_in(seeds[12], 71), 0)
    return dict(grad_cam=grad_cam, cam_diag=cam_diag, precond=precond, point_inv=point_inv, tiles=tiles, tile_block=tile_block, tile_owner=tile_owner, tile_track=tile_track, tile_live=tile_live, covis=covis, pair_row=pair_row, pair_col=pair_col)


highest = lax.Precision.HIGHEST


def invert_points(point_inv, owned_sums):
    count = owned_sums.shape[0]
    coords = owned_sums.reshape(count, 3, -1)
    blocks = point_inv.reshape(count, 3, 3, -1)
    return jnp.sum(blocks * coords[:, None, :, :], axis=2).reshape(count, -1)


def apply_system(vector, cam_diag, point_inv, tiles, tile_block, tile_owner, tile_track, tile_live, covis, pair_row, pair_col):
    rounded = lax.optimization_barrier(vector.astype(jnp.bfloat16)).astype(jnp.float32)
    groups = jnp.arange(N_CAM * N_TRK, dtype=jnp.int32)

    def tile_ids(group_index):
        start = group_index * NT_DEV
        block_ids = (group_index // N_TRK) * CB_DEV + lax.dynamic_slice_in_dim(tile_block, start, NT_DEV, 0)
        owners = lax.dynamic_slice_in_dim(tile_owner, start, NT_DEV, 0)
        track_ids = (owners * N_TRK + group_index % N_TRK) * TT_DEV + lax.dynamic_slice_in_dim(tile_track, start, NT_DEV, 0)
        live_mask = (jnp.arange(NT_DEV, dtype=jnp.int32) < tile_live[group_index]).astype(jnp.float32)
        tile_data = lax.dynamic_slice_in_dim(tiles, start, NT_DEV, 0).astype(jnp.float32)
        return block_ids, track_ids, live_mask, tile_data

    def forward_pass(accum, group_index):
        block_ids, track_ids, live_mask, tile_data = tile_ids(group_index)
        partial_terms = jnp.einsum("tk,tkq->tq", rounded[block_ids], tile_data, precision=highest) * live_mask[:, None]
        return accum.at[track_ids].add(partial_terms), None

    owned_sums, _ = lax.scan(forward_pass, jnp.zeros((NTT, TQ), jnp.float32), groups)
    point_values = lax.optimization_barrier(invert_points(point_inv, owned_sums).astype(jnp.bfloat16)).astype(jnp.float32)

    def backward_pass(accum, group_index):
        block_ids, track_ids, live_mask, tile_data = tile_ids(group_index)
        images = jnp.einsum("tq,tkq->tk", point_values[track_ids], tile_data, precision=highest) * live_mask[:, None]
        return accum.at[block_ids].add(images), None

    schur, _ = lax.scan(backward_pass, jnp.zeros((NB, KB), jnp.float32), groups)

    def pair_pass(accum, group_index):
        start = group_index * NU_DEV
        row_ids = (group_index // N_TRK) * CB_DEV + lax.dynamic_slice_in_dim(pair_row, start, NU_DEV, 0)
        col_ids = lax.dynamic_slice_in_dim(pair_col, start, NU_DEV, 0)
        pair_tiles = lax.dynamic_slice_in_dim(covis, start, NU_DEV, 0).astype(jnp.float32)
        forward = jnp.einsum("pjk,pk->pj", pair_tiles, rounded[col_ids], precision=highest)
        mirrored = jnp.einsum("pjk,pj->pk", pair_tiles, rounded[row_ids], precision=highest)
        return accum.at[row_ids].add(forward).at[col_ids].add(mirrored), None

    coupled, _ = lax.scan(pair_pass, jnp.zeros((NB, KB), jnp.float32), groups)
    return cam_diag * vector + coupled - schur


def reference(grad_cam, cam_diag, precond, point_inv, tiles, tile_block, tile_owner, tile_track, tile_live, covis, pair_row, pair_col):
    step_field = jnp.zeros_like(grad_cam)
    residual = grad_cam
    scaled = precond * residual
    direction = scaled
    inner_now = jnp.sum(residual * scaled)
    for step in range(ITERS):
        image = apply_system(direction, cam_diag, point_inv, tiles, tile_block, tile_owner, tile_track, tile_live, covis, pair_row, pair_col)
        alpha = inner_now / jnp.sum(direction * image)
        step_field = step_field + alpha * direction
        residual = residual - alpha * image
        scaled = precond * residual
        inner_next = jnp.sum(residual * scaled)
        direction = scaled + (inner_next / inner_now) * direction
        inner_now = inner_next
    return step_field, residual
```

```python
import jax
import jax.numpy as jnp
from jax import lax
from jax.experimental import pallas as pl
from jax.experimental.pallas import tpu as pltpu
from jax.sharding import PartitionSpec as P

MESH = pl.DeviceIdType.MESH
F32, BF16, I32 = jnp.float32, jnp.bfloat16, jnp.int32
CAMS = 32
TRKS = 4
TILES = 24
PAIRS = 4
KB = 768
TQ = 384
NN = (((1,), (0,)), ((), ()))
NT = (((1,), (1,)), ((), ()))


def iota(shape, dim):
    return lax.broadcasted_iota(I32, shape, dim)


def hot(mask):
    return jnp.where(mask, 1.0, 0.0).astype(BF16)


def dot(a, b, dims=NN):
    return lax.dot_general(a, b, dims, preferred_element_type=F32)


def total(a):
    return jnp.sum(jnp.sum(a, axis=0, keepdims=True), axis=1, keepdims=True)


def pack(dup):
    low = iota((8, 128), 0) < 4
    return jnp.concatenate(
        [jnp.where(low, dup[:, 256 * j : 256 * j + 128], dup[:, 256 * j + 128 : 256 * j + 256]) for j in range(3)],
        axis=0,
    )


def unpack(packed):
    low = iota((8, 128), 0) < 4
    parts = []
    for j in range(3):
        here = packed[8 * j : 8 * j + 8]
        turned = pltpu.roll(here, 4, 0)
        parts += [jnp.where(low, here, turned), jnp.where(low, turned, here)]
    return jnp.concatenate(parts, axis=1)


def triple(row):
    high = row.astype(BF16).astype(F32)
    rest = row - high
    mid = rest.astype(BF16).astype(F32)
    low = rest - mid
    sub = iota((8, 128), 0)
    return jnp.where(sub == 0, high, jnp.where(sub == 1, mid, jnp.where(sub == 2, low, 0.0)))


def peer_of(me, j):
    def hop(k):
        return jnp.where(k == 2, 3, jnp.where(k == 3, 0, 2 - k))

    z, x, core = me // 8, (me // 2) % 4, me % 2
    return ((z + hop(j // 8)) % 4) * 8 + ((x + hop((j // 2) % 4)) % 4) * 2 + (core + 1 - j % 2) % 2


def kernel(
    grad_ref, diag_ref, prec_ref, inv_ref, tiles_hbm, blk_ref, own_ref, trk_ref, live_ref, covis_hbm, prow_ref, pcol_ref,
    step_ref, res_ref,
    tiles, covis, wide, stack, send_vec, recv_vec, send_mir, recv_mir, send_sum, recv_sum, send_val, recv_val,
    send_tot, recv_tot, to_slots, from_slots, gather_rows, scatter_rows, pick_cols, add_mir,
    tile_sem, covis_sem, send_sem, recv_sem,
):
    me, trk = lax.axis_index("cam"), lax.axis_index("trk")

    def load_tile(i):
        return pltpu.make_async_copy(tiles_hbm.at[i], tiles.at[i], tile_sem.at[i])

    def load_pair(k):
        return pltpu.make_async_copy(covis_hbm.at[k], covis.at[k], covis_sem.at[k])

    barrier = pltpu.get_barrier_semaphore()

    def greet(j, carry):
        pl.semaphore_signal(barrier, inc=1, device_id=(peer_of(me, j), trk), device_id_type=MESH)
        return carry

    lax.fori_loop(0, CAMS - 1, greet, 0)
    for j in range(1, TRKS):
        pl.semaphore_signal(barrier, inc=1, device_id=(me, (trk + j) % TRKS), device_id_type=MESH)

    def start_tile(i, carry):
        load_tile(i).start()
        return carry

    lax.fori_loop(0, TILES, start_tile, 0)
    for k in range(PAIRS):
        load_pair(k).start()

    def send_all(src, dst, rows, sem, own_part):
        def step(j, carry):
            peer = peer_of(me, j)
            part = src.at[pl.ds(pl.multiple_of(peer * rows, rows), rows)] if own_part else src
            pltpu.make_async_remote_copy(
                part,
                dst.at[pl.ds(pl.multiple_of(me * rows, rows), rows)],
                send_sem.at[sem],
                recv_sem.at[sem],
                device_id=(peer, trk),
                device_id_type=MESH,
            ).start()
            return carry

        lax.fori_loop(0, CAMS - 1, step, 0)

    def wait_all(dst, rows, sem, sems):
        part = dst.at[pl.ds(0, (CAMS - 1) * rows)]
        pltpu.make_async_copy(part, part, sems.at[sem]).wait()

    def mine(rows):
        return pl.ds(pl.multiple_of(me * rows, rows), rows)

    def doubled(ref):
        value = ref[...]
        return jnp.concatenate([value, value], axis=0)

    grad, diag, prec = doubled(grad_ref), doubled(diag_ref), doubled(prec_ref)
    first = prec * grad

    lane = iota((1, 128), 1)
    lane32 = lane & 31
    eye = iota((128, 128), 0) == iota((128, 128), 1)

    def to_col(row):
        return jnp.sum(jnp.where(eye, row, 0.0), axis=1, keepdims=True)

    owner = jnp.full((1, 128), -1, I32)
    track = jnp.zeros((1, 128), I32)
    block = jnp.full((1, 128), -1, I32)
    for i in range(TILES):
        here = lane32 == i
        owner = jnp.where(here, own_ref[i], owner)
        track = jnp.where(here, trk_ref[i], track)
        block = jnp.where(here, blk_ref[i], block)
    owner = jnp.where(lane32 < live_ref[0], owner, -1).astype(F32)
    owner_col = to_col(owner)
    track_col = to_col(track.astype(F32))
    block_col = to_col(block.astype(F32))
    earlier = (owner_col[:32] == owner) & (iota((32, 128), 0) < lane32) & (owner >= 0.0)
    rank = jnp.sum(jnp.where(earlier, 1.0, 0.0), axis=0, keepdims=True)
    rank_col = to_col(rank)
    slot = jnp.where(
        (owner >= 0.0) & (lane < 96), owner * 16.0 + (lane >> 5).astype(F32) * 4.0 + rank, -1.0
    )
    slot_col = to_col(slot)
    slot_of = jnp.where(owner_col >= 0.0, owner_col * 4.0 + rank_col, -1.0)[:32]
    table = jnp.sum(
        jnp.where(slot_of == iota((32, 128), 1).astype(F32), track_col[:32] + 1.0, 0.0), axis=0, keepdims=True
    )
    pair_cols = jnp.zeros((1, 128), I32)
    for k in range(PAIRS):
        pair_cols = jnp.where((lane & 3) == k, pcol_ref[k], pair_cols)
    sub8 = iota((8, 128), 0)
    routes = jnp.where(sub8 == 0, table, jnp.where(sub8 == 1, pair_cols.astype(F32), 0.0))

    def pack_send(vec, extra, send, recv, sem):
        message = jnp.concatenate([pack(vec), extra], axis=0).astype(BF16)
        send[...] = message
        recv[mine(32), :] = message
        send_all(send, recv, 32, sem, False)

    pl.semaphore_wait(barrier, CAMS - 1 + TRKS - 1)
    pack_send(first, routes, send_vec.at[0], recv_vec.at[0], 0)

    to_slots[...] = hot(iota((512, 128), 0).astype(F32) == slot)
    extra_rows = iota((128, 512), 0) - 96
    from_slots[...] = hot(
        (iota((128, 512), 1).astype(F32) == slot_col)
        | ((extra_rows >= 0) & (extra_rows < 3) & ((iota((128, 512), 1) & 15) == 12 + extra_rows))
    )
    row64 = iota((64, 1), 0)
    base = jnp.zeros((64, 1), I32)
    for k in range(PAIRS):
        base = jnp.where((row64 & 3) == k, (pcol_ref[k] // 4) * 32 + pcol_ref[k] % 4, base)
    base = base + (row64 >> 3) * 4
    wide_lane = iota((64, 1024), 1)
    pick_cols[...] = hot(
        ((row64 < 48) & (wide_lane == base)) | ((row64 >= 48) & (row64 < 56) & ((wide_lane & 31) == row64 - 24))
    )
    stack[...] = jnp.zeros((128, 128), F32)
    rows8 = iota((8, 1), 0)
    prow_col = jnp.zeros((8, 1), I32)
    for k in range(PAIRS):
        prow_col = jnp.where((rows8 & 3) == k, prow_ref[k], prow_col)
    rows_wide = iota((8, KB), 0)
    rows_tq = iota((8, TQ), 0)

    def unstack(rows, at, count):
        return jnp.concatenate([rows[at * j : at * j + 8] for j in range(count)], axis=1)

    def forward(vec, load):
        picked = jnp.zeros((32, KB), F32)
        for b in range(4):
            picked = jnp.where(block_col[:32] == b, vec[b : b + 1], picked)
        wide[...] = picked

        def group(g, carry):
            here = wide[pl.ds(pl.multiple_of(g * 8, 8), 8), :]
            out = jnp.zeros((8, TQ), F32)
            for r in range(8):
                if load:
                    load_tile(g * 8 + r).wait()
                out = out + dot(jnp.where(rows_wide == r, here, 0.0).astype(BF16), tiles[g * 8 + r])
            for j in range(3):
                stack[pl.ds(pl.multiple_of(j * 32 + g * 8, 8), 8), :] = out[:, 128 * j : 128 * j + 128]
            return carry

        lax.fori_loop(0, TILES // 8, group, 0)

    def couple(vec):
        rows = jnp.zeros((8, KB), F32)
        for b in range(4):
            rows = jnp.where(prow_col == b, vec[b : b + 1], rows)
        mirrored = jnp.zeros((8, KB), F32)
        for k in range(PAIRS):
            mirrored = mirrored + dot(jnp.where((rows_wide & 3) == k, rows, 0.0).astype(BF16), covis[k])
        return mirrored

    def couple_rows(cols):
        out = jnp.zeros((8, KB), F32)
        for k in range(PAIRS):
            lhs = jnp.where((rows_wide & 3) == prow_ref[k], cols[k : k + 1], 0.0).astype(BF16)
            out = out + dot(lhs, covis[k], NT)
        return out

    def backward(values, start):
        out = start
        for g in range(TILES // 8):
            here = jnp.concatenate([values[32 * j + 8 * g : 32 * j + 8 * g + 8] for j in range(3)], axis=1)
            for r in range(8):
                lhs = jnp.where((rows_tq & 3) == blk_ref[g * 8 + r], here[r : r + 1], 0.0).astype(BF16)
                out = out - dot(lhs, tiles[g * 8 + r], NT)
        return out

    def points(sums):
        parts = []
        for a in range(3):
            part = jnp.zeros((16, 128), F32)
            for e in range(3):
                part = part + inv_ref[3 * a + e] * sums[16 * e : 16 * e + 16]
            parts.append(part)
        return jnp.concatenate(parts, axis=0)

    forward(first, True)
    send_sum[0] = dot(to_slots[...], stack[...].astype(BF16)).astype(BF16)
    recv_sum[0, mine(16), :] = send_sum[0, mine(16), :]
    send_all(send_sum.at[0], recv_sum.at[0], 16, 1, True)

    wait_all(recv_vec.at[0], 32, 0, recv_sem)
    got = recv_vec[0]
    cols = unstack(dot(pick_cols[...], got), 8, 6)
    select = iota((64, 1024), 0)
    source = iota((64, 1024), 1)
    tables = dot(hot(source == (select & 31) * 32 + 24 + (select >> 5)), got)
    mine4 = dot(tables[:32].astype(BF16), hot(iota((128, 128), 0) == me * 4 + (iota((128, 128), 1) & 3)))
    row_codes, col_codes = [], []
    sub32, lane32x = iota((32, 128), 0), iota((32, 128), 1)
    chunk = (lane >> 2) & 3
    for q in range(4):
        value = jnp.sum(jnp.where(sub32 == 8 * q + (lane32x >> 4), mine4, 0.0), axis=0, keepdims=True)
        code = jnp.where((value > 0.0) & (chunk < 3), chunk.astype(F32) * 16.0 + value - 1.0, -1.0)
        row_codes.append(code)
        code = jnp.where((chunk == 3) & ((lane & 3) < 3), 48.0 + (lane & 3).astype(F32), code)
        col_codes.append(to_col(code))
    gather_rows[...] = hot(iota((48, 512), 0).astype(F32) == jnp.concatenate(row_codes, axis=1))
    scatter_rows[...] = hot(iota((512, 128), 1).astype(F32) == jnp.concatenate(col_codes, axis=0))
    mir_codes = []
    part = (lane >> 2) & 7
    for q in range(8):
        value = jnp.sum(jnp.where(sub32 == 4 * q + (lane32x >> 5), tables[32:], 0.0), axis=0, keepdims=True)
        local = value - (me * 4).astype(F32)
        code = jnp.where((local >= 0.0) & (local < 4.0), part.astype(F32) * 4.0 + local, -1.0)
        mir_codes.append(jnp.where(part < 6, code, (lane & 31).astype(F32)))
    add_mir[...] = hot(iota((32, 1024), 0).astype(F32) == jnp.concatenate(mir_codes, axis=1))

    for k in range(PAIRS):
        load_pair(k).wait()
    mirrored = couple(first)
    pack_send(mirrored, jnp.zeros((8, 128), F32), send_mir.at[0], recv_mir.at[0], 2)

    def owners(sums_recv, vals_send, vals_recv, sem, extra):
        sums = dot(gather_rows[...], sums_recv[...])
        values = points(sums)
        fill = jnp.concatenate([values, extra(sums, values), jnp.zeros((72, 128), F32)], axis=0).astype(BF16)
        vals_send[...] = dot(scatter_rows[...], fill).astype(BF16)
        vals_recv[mine(16), :] = vals_send[mine(16), :]
        send_all(vals_send, vals_recv, 16, sem, True)

    wait_all(recv_sum.at[0], 16, 1, recv_sem)
    quad = total(cols * mirrored) + 0.125 * total(first * diag * first)
    owned_inner = 0.125 * total(grad * first)
    owners(
        recv_sum.at[0],
        send_val.at[0],
        recv_val.at[0],
        3,
        lambda s, v: triple(jnp.where(lane == 0, quad - total(s * v), jnp.where(lane == 1, owned_inner, 0.0))),
    )
    coupled = couple_rows(cols)

    def exchange(message, send, recv, sem):
        send[...] = message
        for j in range(1, TRKS):
            pltpu.make_async_remote_copy(
                send,
                recv.at[trk],
                send_sem.at[sem],
                recv_sem.at[sem],
                device_id=(me, (trk + j) % TRKS),
                device_id_type=MESH,
            ).start()
        recv[trk] = message
        part = recv.at[pl.ds(0, TRKS - 1)]
        pltpu.make_async_copy(part, part, recv_sem.at[sem]).wait()
        return (recv[0] + recv[1]) + (recv[2] + recv[3])

    wait_all(recv_mir.at[0], 32, 2, recv_sem)
    mir = dot(add_mir[...], recv_mir[0])
    wait_all(recv_val.at[0], 16, 3, recv_sem)
    values = dot(from_slots[...], recv_val[0])
    quads = values[96:97] + values[97:98] + values[98:99]
    local = backward(values, coupled)
    message = jnp.concatenate([pack(local) + mir[:24], jnp.where(sub8 == 0, quads, 0.0)], axis=0)
    summed = exchange(message, send_tot.at[0], recv_tot.at[0], 4)
    image = diag * first + unpack(summed[:24])

    dim, rz = summed[24:25, 0:1], summed[24:25, 1:2]
    alpha = rz / dim
    residual = grad - alpha * image

    vec = prec * residual
    inner = jnp.where(lane == 0, 0.5 * total(residual * vec), jnp.where(lane == 1, 0.5 * total(vec * image), 0.0))
    pack_send(vec, triple(inner), send_vec.at[1], recv_vec.at[1], 5)
    forward(vec, False)
    send_sum[1] = dot(to_slots[...], stack[...].astype(BF16)).astype(BF16)
    recv_sum[1, mine(16), :] = send_sum[1, mine(16), :]
    send_all(send_sum.at[1], recv_sum.at[1], 16, 6, True)

    wait_all(recv_vec.at[1], 32, 5, recv_sem)
    got = dot(pick_cols[...], recv_vec[1])
    cols = unstack(got, 8, 6)
    inners = got[48:49] + got[49:50] + got[50:51]
    fresh, cross = inners[:, 0:1], inners[:, 1:2]
    beta = fresh / rz
    direction = vec + beta * first
    mirrored = couple(vec)
    pack_send(mirrored, jnp.zeros((8, 128), F32), send_mir.at[1], recv_mir.at[1], 7)
    quad = total(cols * mirrored) + 0.125 * total(vec * diag * vec)

    wait_all(recv_sum.at[1], 16, 6, recv_sem)
    owners(
        recv_sum.at[1],
        send_val.at[1],
        recv_val.at[1],
        8,
        lambda s, v: triple(jnp.where(lane == 0, quad - total(s * v), 0.0)),
    )
    coupled = couple_rows(cols)
    wait_all(recv_mir.at[1], 32, 7, recv_sem)
    mir = dot(add_mir[...], recv_mir[1])
    wait_all(recv_val.at[1], 16, 8, recv_sem)
    values = dot(from_slots[...], recv_val[1])
    quads = values[96:97] + values[97:98] + values[98:99]
    local = backward(values, coupled)
    message = jnp.concatenate(
        [pack(local) + mir[:24], jnp.where(sub8 == 0, quads, 0.0)], axis=0
    )
    summed = exchange(message, send_tot.at[1], recv_tot.at[1], 9)
    second = diag * vec + unpack(summed[:24]) + beta * image
    curve = summed[24:25, 0:1] + beta * (2.0 * cross + beta * dim)
    alpha_next = fresh / curve
    step_ref[...] = (alpha * first + alpha_next * direction)[:4]
    res_ref[...] = (residual - alpha_next * second)[:4]

    for it in range(2):
        wait_all(recv_vec.at[it], 32, 5 * it, send_sem)
        wait_all(recv_sum.at[it], 16, 5 * it + 1, send_sem)
        wait_all(recv_mir.at[it], 32, 5 * it + 2, send_sem)
        wait_all(recv_val.at[it], 16, 5 * it + 3, send_sem)
        part = recv_tot.at[it, pl.ds(0, TRKS - 1)]
        pltpu.make_async_copy(part, part, send_sem.at[5 * it + 4]).wait()


def shards(*args):
    args = args[:3] + (jnp.transpose(args[3], (1, 0, 2)),) + args[4:]
    vmem = pl.BlockSpec(memory_space=pltpu.VMEM)
    smem = pl.BlockSpec(memory_space=pltpu.SMEM)
    hbm = pl.BlockSpec(memory_space=pl.ANY)
    out = jax.ShapeDtypeStruct((4, KB), F32)
    return pl.pallas_call(
        kernel,
        out_shape=(out, out),
        in_specs=[vmem, vmem, vmem, vmem, hbm, smem, smem, smem, smem, hbm, smem, smem],
        out_specs=(vmem, vmem),
        scratch_shapes=[
            pltpu.VMEM((TILES, KB, TQ), BF16),
            pltpu.VMEM((PAIRS, KB, KB), BF16),
            pltpu.VMEM((32, KB), F32),
            pltpu.VMEM((128, 128), F32),
            pltpu.VMEM((2, 32, 128), BF16),
            pltpu.VMEM((2, 1024, 128), BF16),
            pltpu.VMEM((2, 32, 128), BF16),
            pltpu.VMEM((2, 1024, 128), BF16),
            pltpu.VMEM((2, 512, 128), BF16),
            pltpu.VMEM((2, 512, 128), BF16),
            pltpu.VMEM((2, 512, 128), BF16),
            pltpu.VMEM((2, 512, 128), BF16),
            pltpu.VMEM((2, 32, 128), F32),
            pltpu.VMEM((2, TRKS, 32, 128), F32),
            pltpu.VMEM((512, 128), BF16),
            pltpu.VMEM((128, 512), BF16),
            pltpu.VMEM((48, 512), BF16),
            pltpu.VMEM((512, 128), BF16),
            pltpu.VMEM((64, 1024), BF16),
            pltpu.VMEM((32, 1024), BF16),
            pltpu.SemaphoreType.DMA((TILES,)),
            pltpu.SemaphoreType.DMA((PAIRS,)),
            pltpu.SemaphoreType.DMA((10,)),
            pltpu.SemaphoreType.DMA((10,)),
        ],
        compiler_params=pltpu.CompilerParams(
            collective_id=1, has_side_effects=True, vmem_limit_bytes=56 * 2**20
        ),
        cost_estimate=pl.CostEstimate(flops=8 * 2 * 2 * 9_400_000, bytes_accessed=19_000_000, transcendentals=0),
        name="cg",
    )(*args)


def solution(mesh):
    vec, both = P("cam", None), ("cam", "trk")
    tile, line = P(both, None, None), P(both)
    in_specs = (vec, vec, vec, tile, tile, line, line, line, line, tile, line, line)
    return jax.shard_map(shards, mesh=mesh, in_specs=in_specs, out_specs=(vec, vec), check_vma=False)
```

```python
import jax
import jax.numpy as jnp
from jax import lax
from jax.experimental import pallas as pl
from jax.experimental.pallas import tpu as pltpu
from jax.sharding import PartitionSpec as P

MESH = pl.DeviceIdType.MESH
F32, BF16, I32 = jnp.float32, jnp.bfloat16, jnp.int32
CAMS = 32
TRKS = 4
TILES = 24
PAIRS = 4
KB = 768
TQ = 384
CHUNK = 4
EARLY = 3
NN = (((1,), (0,)), ((), ()))
NT = (((1,), (1,)), ((), ()))


def iota(shape, dim):
    return lax.broadcasted_iota(I32, shape, dim)


def hot(mask):
    return jnp.where(mask, 1.0, 0.0).astype(BF16)


def dot(a, b, dims=NN):
    return lax.dot_general(a, b, dims, preferred_element_type=F32)


def total(a):
    return jnp.sum(jnp.sum(a, axis=0, keepdims=True), axis=1, keepdims=True)


def pack(dup):
    low = iota((8, 128), 0) < 4
    return jnp.concatenate(
        [jnp.where(low, dup[:, 256 * j : 256 * j + 128], dup[:, 256 * j + 128 : 256 * j + 256]) for j in range(3)],
        axis=0,
    )


def unpack(packed):
    low = iota((8, 128), 0) < 4
    parts = []
    for j in range(3):
        here = packed[8 * j : 8 * j + 8]
        turned = pltpu.roll(here, 4, 0)
        parts += [jnp.where(low, here, turned), jnp.where(low, turned, here)]
    return jnp.concatenate(parts, axis=1)


def triple(row):
    high = row.astype(BF16).astype(F32)
    rest = row - high
    mid = rest.astype(BF16).astype(F32)
    low = rest - mid
    sub = iota((8, 128), 0)
    return jnp.where(sub == 0, high, jnp.where(sub == 1, mid, jnp.where(sub == 2, low, 0.0)))


def kernel(
    grad_hbm, diag_hbm, prec_hbm, inv_hbm, tiles_hbm, blk_hbm, own_hbm, trk_hbm, live_hbm, covis_hbm, prow_hbm, pcol_hbm,
    both_ref,
    tiles, flipped, covis, grad_ref, diag_ref, prec_ref, inv_ref, blk_ref, own_ref, trk_ref, live_ref, prow_ref, pcol_ref,
    wide, stack, send_vec, recv_vec, send_mir, recv_mir, send_sum, recv_sum, send_val, recv_val,
    send_tot, recv_tot, to_slots, from_slots, gather_rows, scatter_rows, pick_cols, add_mir,
    load_sem, tile_sem, covis_sem, send_sem, recv_sem,
):
    me, trk = lax.axis_index("cam"), lax.axis_index("trk")
    core, chip = me % 2, me // 2

    small = [
        pltpu.make_async_copy(src, dst, load_sem.at[i])
        for i, (src, dst) in enumerate(
            (
                (own_hbm, own_ref),
                (trk_hbm, trk_ref),
                (blk_hbm, blk_ref),
                (live_hbm, live_ref),
                (prow_hbm, prow_ref),
                (pcol_hbm, pcol_ref),
                (grad_hbm, grad_ref),
                (diag_hbm, diag_ref),
                (prec_hbm, prec_ref),
                (inv_hbm, inv_ref),
            )
        )
    ]
    for copy in small:
        copy.start()

    def load_chunk(c):
        part = pl.ds(c * CHUNK, CHUNK)
        return pltpu.make_async_copy(tiles_hbm.at[part], tiles.at[part], tile_sem.at[c])

    load_pairs = pltpu.make_async_copy(covis_hbm, covis, covis_sem)
    for c in range(TILES // CHUNK):
        load_chunk(c).start()
    load_pairs.start()

    barrier = pltpu.get_barrier_semaphore()

    def far_first(j):
        m = 31 - j
        return m ^ ((m >> 1) & 10)

    def greet(j, carry):
        pl.semaphore_signal(barrier, inc=1, device_id=(me ^ far_first(j), trk), device_id_type=MESH)
        return carry

    lax.fori_loop(0, CAMS - 1, greet, 0)
    for j in range(1, TRKS):
        pl.semaphore_signal(barrier, inc=1, device_id=(me, trk ^ j), device_id_type=MESH)

    def remote(src, dst, sem, to):
        pltpu.make_async_remote_copy(
            src, dst, send_sem.at[sem], recv_sem.at[sem], device_id=to, device_id_type=MESH
        ).start()

    def wait_rows(ref, rows, sem):
        part = ref.at[pl.ds(0, rows)]
        pltpu.make_async_copy(part, part, sem).wait()

    def exchange_all(src, dst, sem):
        def step(j, carry):
            peer = me ^ far_first(j)
            part = src.at[pl.ds(pl.multiple_of(peer * 16, 16), 16)]
            remote(part, dst.at[pl.ds(pl.multiple_of(me * 16, 16), 16)], sem, (peer, trk))
            return carry

        lax.fori_loop(0, CAMS - 1, step, 0)

    mine = pl.ds(pl.multiple_of(me * 16, 16), 16)
    place = pl.ds(pl.multiple_of(core * 512 + chip * 32, 32), 32)
    half = pl.ds(pl.multiple_of(core * 512, 512), 512)

    def gather_start(message, src, dst, sem):
        src[...] = message
        dst[place, :] = message

        def step(j, carry):
            m = 15 - j
            m = m ^ ((m >> 1) & 5)
            remote(src, dst.at[place], sem, (me ^ (2 * m), trk))
            return carry

        lax.fori_loop(0, CAMS // 2 - 1, step, 0)

    def gather_relay(dst, sem):
        wait_rows(dst, 480, recv_sem.at[sem])
        remote(dst.at[half], dst.at[half], sem + 1, (me ^ 1, trk))

    def gather_end(dst, sem):
        wait_rows(dst, 512, recv_sem.at[sem + 1])

    for copy in small[:-1]:
        copy.wait()

    def doubled(ref):
        value = ref[...]
        return jnp.concatenate([value, value], axis=0)

    grad, diag, prec = doubled(grad_ref), doubled(diag_ref), doubled(prec_ref)
    first = prec * grad

    lane = iota((1, 128), 1)
    lane32 = lane & 31
    eye = iota((128, 128), 0) == iota((128, 128), 1)

    def to_col(row):
        return jnp.sum(jnp.where(eye, row, 0.0), axis=1, keepdims=True)

    owner = jnp.full((1, 128), -1, I32)
    track = jnp.zeros((1, 128), I32)
    block = jnp.full((1, 128), -1, I32)
    for i in range(TILES):
        here = lane32 == i
        owner = jnp.where(here, own_ref[i], owner)
        track = jnp.where(here, trk_ref[i], track)
        block = jnp.where(here, blk_ref[i], block)
    owner = jnp.where(lane32 < live_ref[0], owner, -1).astype(F32)
    owner_col = to_col(owner)
    track_col = to_col(track.astype(F32))
    block_col = to_col(block.astype(F32))
    earlier = (owner_col[:32] == owner) & (iota((32, 128), 0) < lane32) & (owner >= 0.0)
    rank = jnp.sum(jnp.where(earlier, 1.0, 0.0), axis=0, keepdims=True)
    rank_col = to_col(rank)
    slot = jnp.where(
        (owner >= 0.0) & (lane < 96), owner * 16.0 + (lane >> 5).astype(F32) * 4.0 + rank, -1.0
    )
    slot_col = to_col(slot)
    slot_of = jnp.where(owner_col >= 0.0, owner_col * 4.0 + rank_col, -1.0)[:32]
    table = jnp.sum(
        jnp.where(slot_of == iota((32, 128), 1).astype(F32), track_col[:32] + 1.0, 0.0), axis=0, keepdims=True
    )
    pair_cols = jnp.zeros((1, 128), I32)
    for k in range(PAIRS):
        pair_cols = jnp.where((lane & 3) == k, pcol_ref[k], pair_cols)
    sub8 = iota((8, 128), 0)
    routes = jnp.where(sub8 == 0, table, jnp.where(sub8 == 1, pair_cols.astype(F32), 0.0))

    def with_rows(packed, extra):
        return jnp.concatenate([packed, extra], axis=0)

    pl.semaphore_wait(barrier, CAMS - 1 + TRKS - 1)

    gather_start(with_rows(pack(first), routes).astype(BF16), send_vec.at[0], recv_vec.at[0], 0)

    to_slots[...] = hot(iota((512, 128), 0).astype(F32) == slot)
    extra_rows = iota((128, 512), 0) - 96
    from_slots[...] = hot(
        (iota((128, 512), 1).astype(F32) == slot_col)
        | ((extra_rows >= 0) & (extra_rows < 3) & ((iota((128, 512), 1) & 15) == 12 + extra_rows))
    )
    row48 = iota((48, 1), 0)
    base = jnp.zeros((48, 1), I32)
    for k in range(PAIRS):
        cam = pcol_ref[k] // 4
        base = jnp.where((row48 & 3) == k, (cam % 2) * 512 + (cam // 2) * 32 + pcol_ref[k] % 4, base)
    base = base + (row48 >> 3) * 4
    pick_cols[...] = hot(iota((48, 1024), 1) == base)
    stack[...] = jnp.zeros((128, 128), F32)
    rows8 = iota((8, 1), 0)
    prow_col = jnp.zeros((8, 1), I32)
    for k in range(PAIRS):
        prow_col = jnp.where((rows8 & 3) == k, prow_ref[k], prow_col)
    rows_wide = iota((8, KB), 0)
    rows_tq = iota((8, TQ), 0)

    def unstack(rows, at, count):
        return jnp.concatenate([rows[at * j : at * j + 8] for j in range(count)], axis=1)

    def forward(vec, load):
        picked = jnp.zeros((32, KB), F32)
        for b in range(4):
            picked = jnp.where(block_col[:32] == b, vec[b : b + 1], picked)
        wide[...] = picked

        def group(g, carry):
            here = wide[pl.ds(pl.multiple_of(g * 8, 8), 8), :]
            out = jnp.zeros((8, TQ), F32)
            for r in range(8):
                if load and r % CHUNK == 0:
                    load_chunk(g * (8 // CHUNK) + r // CHUNK).wait()
                out = out + dot(jnp.where(rows_wide == r, here, 0.0).astype(BF16), tiles[g * 8 + r])
                if load and r % CHUNK < EARLY:
                    flip(g * 8 + r)
            for j in range(3):
                stack[pl.ds(pl.multiple_of(j * 32 + g * 8, 8), 8), :] = out[:, 128 * j : 128 * j + 128]
            return carry

        lax.fori_loop(0, TILES // 8, group, 0)

    def send_sums(src, dst, sem):
        src[...] = dot(to_slots[...], stack[...].astype(BF16)).astype(BF16)
        dst[mine, :] = src[mine, :]
        exchange_all(src, dst, sem)

    def flip(i):
        flipped[i] = tiles[i].T

    def flip_late(c, carry):
        for r in range(EARLY, CHUNK):
            flip(c * CHUNK + r)
        return carry

    def couple(vec):
        rows = jnp.zeros((8, KB), F32)
        for b in range(4):
            rows = jnp.where(prow_col == b, vec[b : b + 1], rows)
        mirrored = jnp.zeros((8, KB), F32)
        for k in range(PAIRS):
            mirrored = mirrored + dot(jnp.where((rows_wide & 3) == k, rows, 0.0).astype(BF16), covis[k])
        return mirrored

    def couple_rows(cols):
        out = jnp.zeros((8, KB), F32)
        for k in range(PAIRS):
            lhs = jnp.where((rows_wide & 3) == prow_ref[k], cols[k : k + 1], 0.0).astype(BF16)
            out = out + dot(lhs, covis[k], NT)
        return out

    def backward(values, start):
        out = start
        for g in range(TILES // 8):
            here = jnp.concatenate([values[32 * j + 8 * g : 32 * j + 8 * g + 8] for j in range(3)], axis=1)
            for r in range(8):
                lhs = jnp.where((rows_tq & 3) == blk_ref[g * 8 + r], here[r : r + 1], 0.0).astype(BF16)
                out = out - dot(lhs, flipped[g * 8 + r])
        return out

    def points(sums):
        parts = []
        for a in range(3):
            part = jnp.zeros((16, 128), F32)
            for e in range(3):
                part = part + inv_ref[3 * a + e] * sums[16 * e : 16 * e + 16]
            parts.append(part)
        return jnp.concatenate(parts, axis=0)

    def owners(sums_recv, src, dst, sem, own_quad):
        sums = dot(gather_rows[...], sums_recv[...])
        values = points(sums)
        inner = triple(own_quad - jnp.sum(sums * values, axis=0, keepdims=True))
        fill = jnp.concatenate([values, inner, jnp.zeros((72, 128), F32)], axis=0).astype(BF16)
        src[...] = dot(scatter_rows[...], fill).astype(BF16)
        dst[mine, :] = src[mine, :]
        exchange_all(src, dst, sem)

    def quad_row(wide_rows):
        rows = sum(wide_rows[:, 128 * j : 128 * j + 128] for j in range(6))
        return jnp.sum(rows, axis=0, keepdims=True)

    def scalars(*values):
        row = jnp.zeros((1, 128), F32)
        for k, value in enumerate(values):
            row = jnp.where(lane == k, value, row)
        return triple(row)

    def sum_trk(local, mir, values, src, dst, sem):
        quads = values[96:97] + values[97:98] + values[98:99]
        quads = jnp.where(lane == 0, jnp.sum(quads, axis=1, keepdims=True), 0.0)
        inners = mir[24:25] + mir[25:26] + mir[26:27] + quads
        src[...] = with_rows(pack(local) + mir[:24], jnp.where(sub8 == 0, inners, 0.0))
        for j in (2, 1, 3):
            remote(src, dst.at[trk], sem, (me, trk ^ j))
        dst[trk] = src[...]
        wait_rows(dst, TRKS - 1, recv_sem.at[sem])
        return (dst[0] + dst[1]) + (dst[2] + dst[3])

    forward(first, True)
    send_sums(send_sum.at[0], recv_sum.at[0], 2)

    gather_relay(recv_vec.at[0], 0)
    small[-1].wait()
    load_pairs.wait()
    mirrored = couple(first)
    inner = scalars(0.0, 0.125 * total(grad * first))
    gather_start(with_rows(pack(mirrored), inner).astype(BF16), send_mir.at[0], recv_mir.at[0], 3)
    gather_end(recv_vec.at[0], 0)
    got = recv_vec[0]
    cols = unstack(dot(pick_cols[...], got), 8, 6)
    select = iota((64, 1), 0)
    source = jnp.where(select < 32, (select & 1) * 512 + (select >> 1) * 32 + 24, (select & 31) * 32 + 25)
    tables = dot(hot(iota((64, 1024), 1) == source), got)
    mine4 = dot(tables[:32].astype(BF16), hot(iota((128, 128), 0) == me * 4 + (iota((128, 128), 1) & 3)))
    row_codes, col_codes = [], []
    sub32, lane32x = iota((32, 128), 0), iota((32, 128), 1)
    chunk = (lane >> 2) & 3
    for q in range(4):
        value = jnp.sum(jnp.where(sub32 == 8 * q + (lane32x >> 4), mine4, 0.0), axis=0, keepdims=True)
        code = jnp.where((value > 0.0) & (chunk < 3), chunk.astype(F32) * 16.0 + value - 1.0, -1.0)
        row_codes.append(code)
        code = jnp.where((chunk == 3) & ((lane & 3) < 3), 48.0 + (lane & 3).astype(F32), code)
        col_codes.append(to_col(code))
    gather_rows[...] = hot(iota((48, 512), 0).astype(F32) == jnp.concatenate(row_codes, axis=1))
    scatter_rows[...] = hot(iota((512, 128), 1).astype(F32) == jnp.concatenate(col_codes, axis=0))
    mir_codes = []
    part = (lane >> 2) & 7
    for q in range(8):
        value = jnp.sum(jnp.where(sub32 == 4 * q + (lane32x >> 5), tables[32:], 0.0), axis=0, keepdims=True)
        local = value - (me * 4).astype(F32)
        code = jnp.where((local >= 0.0) & (local < 4.0), part.astype(F32) * 4.0 + local, -1.0)
        mir_codes.append(jnp.where(part < 6, code, (lane & 31).astype(F32)))
    add_mir[...] = hot(iota((32, 1024), 0).astype(F32) == jnp.concatenate(mir_codes, axis=1))

    own_quad = quad_row(cols * mirrored + 0.125 * first * diag * first)

    wait_rows(recv_sum.at[0], 496, recv_sem.at[2])
    owners(recv_sum.at[0], send_val.at[0], recv_val.at[0], 5, own_quad)
    gather_relay(recv_mir.at[0], 3)
    coupled = couple_rows(cols)
    lax.fori_loop(0, TILES // CHUNK, flip_late, 0)
    gather_end(recv_mir.at[0], 3)
    mir = dot(add_mir[...], recv_mir[0])
    wait_rows(recv_val.at[0], 496, recv_sem.at[5])
    values = dot(from_slots[...], recv_val[0])
    local = backward(values, coupled)
    summed = sum_trk(local, mir, values, send_tot.at[0], recv_tot.at[0], 6)
    image = diag * first + unpack(summed[:24])
    dim, rz = summed[24:25, 0:1], summed[24:25, 1:2]
    alpha = rz / dim
    residual = grad - alpha * image

    vec = prec * residual
    gather_start(with_rows(pack(vec), jnp.zeros((8, 128), F32)).astype(BF16), send_vec.at[1], recv_vec.at[1], 7)
    forward(vec, False)
    send_sums(send_sum.at[1], recv_sum.at[1], 9)

    gather_relay(recv_vec.at[1], 7)
    mirrored = couple(vec)
    inner = scalars(0.0, 0.125 * total(residual * vec), 0.125 * total(vec * image))
    gather_start(with_rows(pack(mirrored), inner).astype(BF16), send_mir.at[1], recv_mir.at[1], 10)
    gather_end(recv_vec.at[1], 7)
    cols = unstack(dot(pick_cols[...], recv_vec[1]), 8, 6)
    own_quad = quad_row(cols * mirrored + 0.125 * vec * diag * vec)

    wait_rows(recv_sum.at[1], 496, recv_sem.at[9])
    owners(recv_sum.at[1], send_val.at[1], recv_val.at[1], 12, own_quad)
    gather_relay(recv_mir.at[1], 10)
    coupled = couple_rows(cols)
    gather_end(recv_mir.at[1], 10)
    mir = dot(add_mir[...], recv_mir[1])
    wait_rows(recv_val.at[1], 496, recv_sem.at[12])
    values = dot(from_slots[...], recv_val[1])
    local = backward(values, coupled)
    summed = sum_trk(local, mir, values, send_tot.at[1], recv_tot.at[1], 13)
    inners = summed[24:25]
    fresh, cross = inners[:, 1:2], inners[:, 2:3]
    beta = fresh / rz
    second = diag * vec + unpack(summed[:24]) + beta * image
    curve = inners[:, 0:1] + beta * (2.0 * cross + beta * dim)
    alpha_next = fresh / curve
    step = alpha * first + alpha_next * (vec + beta * first)
    both_ref[...] = jnp.where(iota((8, KB), 0) < 4, step, residual - alpha_next * second)

    for it in range(2):
        at = 7 * it
        wait_rows(recv_vec.at[it], 480, send_sem.at[at])
        wait_rows(recv_vec.at[it], 512, send_sem.at[at + 1])
        wait_rows(recv_sum.at[it], 496, send_sem.at[at + 2])
        wait_rows(recv_mir.at[it], 480, send_sem.at[at + 3])
        wait_rows(recv_mir.at[it], 512, send_sem.at[at + 4])
        wait_rows(recv_val.at[it], 496, send_sem.at[at + 5])
        wait_rows(recv_tot.at[it], TRKS - 1, send_sem.at[at + 6])


def shards(*args):
    args = args[:3] + (jnp.transpose(args[3], (1, 0, 2)),) + args[4:]
    vmem = pl.BlockSpec(memory_space=pltpu.VMEM)
    hbm = pl.BlockSpec(memory_space=pl.ANY)
    out = jax.ShapeDtypeStruct((8, KB), F32)
    vec = pltpu.VMEM((4, KB), F32)
    both = pl.pallas_call(
        kernel,
        out_shape=out,
        in_specs=[hbm] * 12,
        out_specs=vmem,
        scratch_shapes=[
            pltpu.VMEM((TILES, KB, TQ), BF16),
            pltpu.VMEM((TILES, TQ, KB), BF16),
            pltpu.VMEM((PAIRS, KB, KB), BF16),
            vec,
            vec,
            vec,
            pltpu.VMEM((9, 16, 128), F32),
            pltpu.SMEM((TILES,), I32),
            pltpu.SMEM((TILES,), I32),
            pltpu.SMEM((TILES,), I32),
            pltpu.SMEM((1,), I32),
            pltpu.SMEM((PAIRS,), I32),
            pltpu.SMEM((PAIRS,), I32),
            pltpu.VMEM((32, KB), F32),
            pltpu.VMEM((128, 128), F32),
            pltpu.VMEM((2, 32, 128), BF16),
            pltpu.VMEM((2, 1024, 128), BF16),
            pltpu.VMEM((2, 32, 128), BF16),
            pltpu.VMEM((2, 1024, 128), BF16),
            pltpu.VMEM((2, 512, 128), BF16),
            pltpu.VMEM((2, 512, 128), BF16),
            pltpu.VMEM((2, 512, 128), BF16),
            pltpu.VMEM((2, 512, 128), BF16),
            pltpu.VMEM((2, 32, 128), F32),
            pltpu.VMEM((2, TRKS, 32, 128), F32),
            pltpu.VMEM((512, 128), BF16),
            pltpu.VMEM((128, 512), BF16),
            pltpu.VMEM((48, 512), BF16),
            pltpu.VMEM((512, 128), BF16),
            pltpu.VMEM((48, 1024), BF16),
            pltpu.VMEM((32, 1024), BF16),
            pltpu.SemaphoreType.DMA((10,)),
            pltpu.SemaphoreType.DMA((TILES // CHUNK,)),
            pltpu.SemaphoreType.DMA,
            pltpu.SemaphoreType.DMA((14,)),
            pltpu.SemaphoreType.DMA((14,)),
        ],
        compiler_params=pltpu.CompilerParams(
            collective_id=1, has_side_effects=True, vmem_limit_bytes=56 * 2**20
        ),
        cost_estimate=pl.CostEstimate(flops=300_000_000, bytes_accessed=19_000_000, transcendentals=0),
        name="cg",
    )(*args)
    return both[:4], both[4:]


def solution(mesh):
    vec, both = P("cam", None), ("cam", "trk")
    tile, line = P(both, None, None), P(both)
    in_specs = (vec, vec, vec, tile, tile, line, line, line, line, tile, line, line)
    return jax.shard_map(shards, mesh=mesh, in_specs=in_specs, out_specs=(vec, vec), check_vma=False)
```

```python
import jax
import jax.numpy as jnp
from jax import lax
from jax.experimental import pallas as pl
from jax.experimental.pallas import tpu as pltpu
from jax.sharding import PartitionSpec as P

MESH = pl.DeviceIdType.MESH
F32, BF16, I32 = jnp.float32, jnp.bfloat16, jnp.int32
CAMS = 32
TRKS = 4
TILES = 24
PAIRS = 4
KB = 768
TQ = 384
CHUNK = 4
EARLY, MID, LATE = 3, 3, 3
NN = (((1,), (0,)), ((), ()))
NT = (((1,), (1,)), ((), ()))


def iota(shape, dim):
    return lax.broadcasted_iota(I32, shape, dim)


def hot(mask):
    return jnp.where(mask, 1.0, 0.0).astype(BF16)


def dot(a, b, dims=NN):
    return lax.dot_general(a, b, dims, preferred_element_type=F32)


def total(a):
    return jnp.sum(jnp.sum(a, axis=0, keepdims=True), axis=1, keepdims=True)


def pack(dup):
    low = iota((8, 128), 0) < 4
    return jnp.concatenate(
        [jnp.where(low, dup[:, 256 * j : 256 * j + 128], dup[:, 256 * j + 128 : 256 * j + 256]) for j in range(3)],
        axis=0,
    )


def unpack(packed):
    low = iota((8, 128), 0) < 4
    parts = []
    for j in range(3):
        here = packed[8 * j : 8 * j + 8]
        turned = pltpu.roll(here, 4, 0)
        parts += [jnp.where(low, here, turned), jnp.where(low, turned, here)]
    return jnp.concatenate(parts, axis=1)


def triple(row):
    high = row.astype(BF16).astype(F32)
    rest = row - high
    mid = rest.astype(BF16).astype(F32)
    low = rest - mid
    sub = iota((8, 128), 0)
    return jnp.where(sub == 0, high, jnp.where(sub == 1, mid, jnp.where(sub == 2, low, 0.0)))


def kernel(
    grad_hbm, diag_hbm, prec_hbm, inv_hbm, tiles_hbm, blk_hbm, own_hbm, trk_hbm, live_hbm, covis_hbm, prow_hbm, pcol_hbm,
    both_ref,
    tiles, flipped, covis, grad_ref, diag_ref, prec_ref, inv_ref, blk_ref, own_ref, trk_ref, live_ref, prow_ref, pcol_ref,
    wide, stack, send_vec, recv_vec, send_mir, recv_mir, send_sum, recv_sum, send_val, recv_val,
    send_tot, recv_tot, to_slots, from_slots, gather_rows, scatter_rows, pick_cols, add_mir,
    load_sem, tile_sem, covis_sem, send_sem, recv_sem,
):
    me, trk = lax.axis_index("cam"), lax.axis_index("trk")
    core, chip = me % 2, me // 2

    small = [
        pltpu.make_async_copy(src, dst, load_sem.at[i])
        for i, (src, dst) in enumerate(
            (
                (own_hbm, own_ref),
                (trk_hbm, trk_ref),
                (blk_hbm, blk_ref),
                (live_hbm, live_ref),
                (prow_hbm, prow_ref),
                (pcol_hbm, pcol_ref),
                (grad_hbm, grad_ref),
                (diag_hbm, diag_ref),
                (prec_hbm, prec_ref),
                (inv_hbm, inv_ref),
            )
        )
    ]
    for copy in small[:-1]:
        copy.start()

    def load_chunk(c):
        part = pl.ds(c * CHUNK, CHUNK)
        return pltpu.make_async_copy(tiles_hbm.at[part], tiles.at[part], tile_sem.at[c])

    load_pairs = pltpu.make_async_copy(covis_hbm, covis, covis_sem)

    barrier = pltpu.get_barrier_semaphore()

    def far_first(j):
        m = 31 - j
        return m ^ ((m >> 1) & 10)

    def greet(j, carry):
        pl.semaphore_signal(barrier, inc=1, device_id=(me ^ far_first(j), trk), device_id_type=MESH)
        return carry

    lax.fori_loop(0, CAMS - 1, greet, 0)
    for j in range(1, TRKS):
        pl.semaphore_signal(barrier, inc=1, device_id=(me, trk ^ j), device_id_type=MESH)
    for c in range(TILES // CHUNK):
        load_chunk(c).start()
    small[-1].start()
    load_pairs.start()

    def remote(src, dst, sem, to):
        pltpu.make_async_remote_copy(
            src, dst, send_sem.at[sem], recv_sem.at[sem], device_id=to, device_id_type=MESH
        ).start()

    def wait_rows(ref, rows, sem):
        part = ref.at[pl.ds(0, rows)]
        pltpu.make_async_copy(part, part, sem).wait()

    def exchange_all(src, dst, sem):
        def step(j, carry):
            peer = me ^ far_first(j)
            part = src.at[pl.ds(pl.multiple_of(peer * 16, 16), 16)]
            remote(part, dst.at[pl.ds(pl.multiple_of(me * 16, 16), 16)], sem, (peer, trk))
            return carry

        lax.fori_loop(0, CAMS - 1, step, 0)

    mine = pl.ds(pl.multiple_of(me * 16, 16), 16)
    place = pl.ds(pl.multiple_of(core * 512 + chip * 32, 32), 32)
    half = pl.ds(pl.multiple_of(core * 512, 512), 512)

    def gather_start(message, src, dst, sem):
        src[...] = message
        dst[place, :] = message

        def step(j, carry):
            m = 15 - j
            m = m ^ ((m >> 1) & 5)
            remote(src, dst.at[place], sem, (me ^ (2 * m), trk))
            return carry

        lax.fori_loop(0, CAMS // 2 - 1, step, 0)

    def gather_relay(dst, sem):
        wait_rows(dst, 480, recv_sem.at[sem])
        remote(dst.at[half], dst.at[half], sem + 1, (me ^ 1, trk))

    def gather_end(dst, sem):
        wait_rows(dst, 512, recv_sem.at[sem + 1])

    for copy in small[:-1]:
        copy.wait()

    def doubled(ref):
        value = ref[...]
        return jnp.concatenate([value, value], axis=0)

    grad, diag, prec = doubled(grad_ref), doubled(diag_ref), doubled(prec_ref)
    first = prec * grad

    lane = iota((1, 128), 1)
    lane32 = lane & 31
    eye = iota((128, 128), 0) == iota((128, 128), 1)

    def to_col(row):
        return jnp.sum(jnp.where(eye, row, 0.0), axis=1, keepdims=True)

    owner = jnp.full((1, 128), -1, I32)
    track = jnp.zeros((1, 128), I32)
    block = jnp.full((1, 128), -1, I32)
    for i in range(TILES):
        here = lane32 == i
        owner = jnp.where(here, own_ref[i], owner)
        track = jnp.where(here, trk_ref[i], track)
        block = jnp.where(here, blk_ref[i], block)
    owner = jnp.where(lane32 < live_ref[0], owner, -1).astype(F32)
    owner_col = to_col(owner)
    track_col = to_col(track.astype(F32))
    block_col = to_col(block.astype(F32))
    earlier = (owner_col[:32] == owner) & (iota((32, 128), 0) < lane32) & (owner >= 0.0)
    rank = jnp.sum(jnp.where(earlier, 1.0, 0.0), axis=0, keepdims=True)
    rank_col = to_col(rank)
    slot = jnp.where(
        (owner >= 0.0) & (lane < 96), owner * 16.0 + (lane >> 5).astype(F32) * 4.0 + rank, -1.0
    )
    slot_col = to_col(slot)
    slot_of = jnp.where(owner_col >= 0.0, owner_col * 4.0 + rank_col, -1.0)[:32]
    table = jnp.sum(
        jnp.where(slot_of == iota((32, 128), 1).astype(F32), track_col[:32] + 1.0, 0.0), axis=0, keepdims=True
    )
    pair_cols = jnp.zeros((1, 128), I32)
    for k in range(PAIRS):
        pair_cols = jnp.where((lane & 3) == k, pcol_ref[k], pair_cols)
    sub8 = iota((8, 128), 0)
    routes = jnp.where(sub8 == 0, table, jnp.where(sub8 == 1, pair_cols.astype(F32), 0.0))

    def with_rows(packed, extra):
        return jnp.concatenate([packed, extra], axis=0)

    pl.semaphore_wait(barrier, CAMS - 1 + TRKS - 1)

    gather_start(with_rows(pack(first), routes).astype(BF16), send_vec.at[0], recv_vec.at[0], 0)

    to_slots[...] = hot(iota((512, 128), 0).astype(F32) == slot)
    extra_rows = iota((128, 512), 0) - 96
    from_slots[...] = hot(
        (iota((128, 512), 1).astype(F32) == slot_col)
        | ((extra_rows >= 0) & (extra_rows < 3) & ((iota((128, 512), 1) & 15) == 12 + extra_rows))
    )
    row48 = iota((48, 1), 0)
    base = jnp.zeros((48, 1), I32)
    for k in range(PAIRS):
        cam = pcol_ref[k] // 4
        base = jnp.where((row48 & 3) == k, (cam % 2) * 512 + (cam // 2) * 32 + pcol_ref[k] % 4, base)
    base = base + (row48 >> 3) * 4
    pick_cols[...] = hot(iota((48, 1024), 1) == base)
    stack[...] = jnp.zeros((128, 128), F32)
    rows8 = iota((8, 1), 0)
    prow_col = jnp.zeros((8, 1), I32)
    for k in range(PAIRS):
        prow_col = jnp.where((rows8 & 3) == k, prow_ref[k], prow_col)
    rows_wide = iota((8, KB), 0)
    rows_tq = iota((8, TQ), 0)

    def unstack(rows, at, count):
        return jnp.concatenate([rows[at * j : at * j + 8] for j in range(count)], axis=1)

    def forward(vec, load):
        picked = jnp.zeros((32, KB), F32)
        for b in range(4):
            picked = jnp.where(block_col[:32] == b, vec[b : b + 1], picked)
        wide[...] = picked

        def group(g, carry):
            here = wide[pl.ds(pl.multiple_of(g * 8, 8), 8), :]
            out = jnp.zeros((8, TQ), F32)
            for r in range(8):
                if load and r % CHUNK == 0:
                    load_chunk(g * (8 // CHUNK) + r // CHUNK).wait()
                out = out + dot(jnp.where(rows_wide == r, here, 0.0).astype(BF16), tiles[g * 8 + r])
                if load and r % CHUNK < EARLY:
                    flip(g * 8 + r)
            for j in range(3):
                stack[pl.ds(pl.multiple_of(j * 32 + g * 8, 8), 8), :] = out[:, 128 * j : 128 * j + 128]
            return carry

        lax.fori_loop(0, TILES // 8, group, 0)

    def send_sums(src, dst, sem):
        src[...] = dot(to_slots[...], stack[...].astype(BF16)).astype(BF16)
        dst[mine, :] = src[mine, :]
        exchange_all(src, dst, sem)

    def flip(i):
        flipped[i] = tiles[i].T

    chunks = TILES // CHUNK
    left = TILES - chunks * EARLY

    def flip_left(start, end):
        def one(k, carry):
            flip((k % chunks) * CHUNK + EARLY + k // chunks)
            return carry

        if start < end:
            lax.fori_loop(start, end, one, 0)

    def couple(vec):
        rows = jnp.zeros((8, KB), F32)
        for b in range(4):
            rows = jnp.where(prow_col == b, vec[b : b + 1], rows)
        mirrored = jnp.zeros((8, KB), F32)
        for k in range(PAIRS):
            mirrored = mirrored + dot(jnp.where((rows_wide & 3) == k, rows, 0.0).astype(BF16), covis[k])
        return mirrored

    def couple_rows(cols):
        out = jnp.zeros((8, KB), F32)
        for k in range(PAIRS):
            lhs = jnp.where((rows_wide & 3) == prow_ref[k], cols[k : k + 1], 0.0).astype(BF16)
            out = out + dot(lhs, covis[k], NT)
        return out

    def backward(values, start, done):
        out = start
        for g in range(TILES // 8):
            here = jnp.concatenate([values[32 * j + 8 * g : 32 * j + 8 * g + 8] for j in range(3)], axis=1)
            for r in range(8):
                lhs = jnp.where((rows_tq & 3) == blk_ref[g * 8 + r], here[r : r + 1], 0.0).astype(BF16)
                if (r % CHUNK - EARLY) * chunks + (g * 8 + r) // CHUNK < done:
                    out = out - dot(lhs, flipped[g * 8 + r])
                else:
                    out = out - dot(lhs, tiles[g * 8 + r], NT)
        return out

    def points(sums):
        parts = []
        for a in range(3):
            part = jnp.zeros((16, 128), F32)
            for e in range(3):
                part = part + inv_ref[3 * a + e] * sums[16 * e : 16 * e + 16]
            parts.append(part)
        return jnp.concatenate(parts, axis=0)

    def owners(sums_recv, src, dst, sem, own_quad):
        sums = dot(gather_rows[...], sums_recv[...])
        values = points(sums)
        inner = triple(own_quad - jnp.sum(sums * values, axis=0, keepdims=True))
        fill = jnp.concatenate([values, inner, jnp.zeros((72, 128), F32)], axis=0).astype(BF16)
        src[...] = dot(scatter_rows[...], fill).astype(BF16)
        dst[mine, :] = src[mine, :]
        exchange_all(src, dst, sem)

    def quad_row(wide_rows):
        rows = sum(wide_rows[:, 128 * j : 128 * j + 128] for j in range(6))
        return jnp.sum(rows, axis=0, keepdims=True)

    def scalars(*values):
        row = jnp.zeros((1, 128), F32)
        for k, value in enumerate(values):
            row = jnp.where(lane == k, value, row)
        return triple(row)

    def sum_trk(local, mir, values, src, dst, sem, meanwhile):
        quads = values[96:97] + values[97:98] + values[98:99]
        quads = jnp.where(lane == 0, jnp.sum(quads, axis=1, keepdims=True), 0.0)
        inners = mir[24:25] + mir[25:26] + mir[26:27] + quads
        src[...] = with_rows(pack(local) + mir[:24], jnp.where(sub8 == 0, inners, 0.0))
        for j in (2, 1, 3):
            remote(src, dst.at[trk], sem, (me, trk ^ j))
        dst[trk] = src[...]
        meanwhile()
        wait_rows(dst, TRKS - 1, recv_sem.at[sem])
        return (dst[0] + dst[1]) + (dst[2] + dst[3])

    forward(first, True)
    send_sums(send_sum.at[0], recv_sum.at[0], 2)

    gather_relay(recv_vec.at[0], 0)
    small[-1].wait()
    load_pairs.wait()
    mirrored = couple(first)
    inner = scalars(0.0, 0.125 * total(grad * first))
    gather_start(with_rows(pack(mirrored), inner).astype(BF16), send_mir.at[0], recv_mir.at[0], 3)
    gather_end(recv_vec.at[0], 0)
    got = recv_vec[0]
    cols = unstack(dot(pick_cols[...], got), 8, 6)
    select = iota((64, 1), 0)
    source = jnp.where(select < 32, (select & 1) * 512 + (select >> 1) * 32 + 24, (select & 31) * 32 + 25)
    tables = dot(hot(iota((64, 1024), 1) == source), got)
    mine4 = dot(tables[:32].astype(BF16), hot(iota((128, 128), 0) == me * 4 + (iota((128, 128), 1) & 3)))
    row_codes, col_codes = [], []
    sub32, lane32x = iota((32, 128), 0), iota((32, 128), 1)
    chunk = (lane >> 2) & 3
    for q in range(4):
        value = jnp.sum(jnp.where(sub32 == 8 * q + (lane32x >> 4), mine4, 0.0), axis=0, keepdims=True)
        code = jnp.where((value > 0.0) & (chunk < 3), chunk.astype(F32) * 16.0 + value - 1.0, -1.0)
        row_codes.append(code)
        code = jnp.where((chunk == 3) & ((lane & 3) < 3), 48.0 + (lane & 3).astype(F32), code)
        col_codes.append(to_col(code))
    gather_rows[...] = hot(iota((48, 512), 0).astype(F32) == jnp.concatenate(row_codes, axis=1))
    scatter_rows[...] = hot(iota((512, 128), 1).astype(F32) == jnp.concatenate(col_codes, axis=0))
    mir_codes = []
    part = (lane >> 2) & 7
    for q in range(8):
        value = jnp.sum(jnp.where(sub32 == 4 * q + (lane32x >> 5), tables[32:], 0.0), axis=0, keepdims=True)
        local = value - (me * 4).astype(F32)
        code = jnp.where((local >= 0.0) & (local < 4.0), part.astype(F32) * 4.0 + local, -1.0)
        mir_codes.append(jnp.where(part < 6, code, (lane & 31).astype(F32)))
    add_mir[...] = hot(iota((32, 1024), 0).astype(F32) == jnp.concatenate(mir_codes, axis=1))

    own_quad = quad_row(cols * mirrored + 0.125 * first * diag * first)

    flip_left(0, MID)
    wait_rows(recv_sum.at[0], 496, recv_sem.at[2])
    owners(recv_sum.at[0], send_val.at[0], recv_val.at[0], 5, own_quad)
    gather_relay(recv_mir.at[0], 3)
    coupled = couple_rows(cols)
    flip_left(MID, MID + LATE)
    gather_end(recv_mir.at[0], 3)
    mir = dot(add_mir[...], recv_mir[0])
    wait_rows(recv_val.at[0], 496, recv_sem.at[5])
    values = dot(from_slots[...], recv_val[0])
    local = backward(values, coupled, MID + LATE)
    summed = sum_trk(local, mir, values, send_tot.at[0], recv_tot.at[0], 6, lambda: flip_left(MID + LATE, left))
    image = diag * first + unpack(summed[:24])
    dim, rz = summed[24:25, 0:1], summed[24:25, 1:2]
    alpha = rz / dim
    residual = grad - alpha * image

    vec = prec * residual
    gather_start(with_rows(pack(vec), jnp.zeros((8, 128), F32)).astype(BF16), send_vec.at[1], recv_vec.at[1], 7)
    forward(vec, False)
    send_sums(send_sum.at[1], recv_sum.at[1], 9)

    gather_relay(recv_vec.at[1], 7)
    mirrored = couple(vec)
    inner = scalars(0.0, 0.125 * total(residual * vec), 0.125 * total(vec * image))
    gather_start(with_rows(pack(mirrored), inner).astype(BF16), send_mir.at[1], recv_mir.at[1], 10)
    gather_end(recv_vec.at[1], 7)
    cols = unstack(dot(pick_cols[...], recv_vec[1]), 8, 6)
    own_quad = quad_row(cols * mirrored + 0.125 * vec * diag * vec)

    wait_rows(recv_sum.at[1], 496, recv_sem.at[9])
    owners(recv_sum.at[1], send_val.at[1], recv_val.at[1], 12, own_quad)
    gather_relay(recv_mir.at[1], 10)
    coupled = couple_rows(cols)
    gather_end(recv_mir.at[1], 10)
    mir = dot(add_mir[...], recv_mir[1])
    wait_rows(recv_val.at[1], 496, recv_sem.at[12])
    values = dot(from_slots[...], recv_val[1])
    local = backward(values, coupled, left)
    summed = sum_trk(local, mir, values, send_tot.at[1], recv_tot.at[1], 13, lambda: None)
    inners = summed[24:25]
    fresh, cross = inners[:, 1:2], inners[:, 2:3]
    beta = fresh / rz
    second = diag * vec + unpack(summed[:24]) + beta * image
    curve = inners[:, 0:1] + beta * (2.0 * cross + beta * dim)
    alpha_next = fresh / curve
    step = alpha * first + alpha_next * (vec + beta * first)
    both_ref[...] = jnp.where(iota((8, KB), 0) < 4, step, residual - alpha_next * second)

    for it in range(2):
        at = 7 * it
        wait_rows(recv_vec.at[it], 480, send_sem.at[at])
        wait_rows(recv_vec.at[it], 512, send_sem.at[at + 1])
        wait_rows(recv_sum.at[it], 496, send_sem.at[at + 2])
        wait_rows(recv_mir.at[it], 480, send_sem.at[at + 3])
        wait_rows(recv_mir.at[it], 512, send_sem.at[at + 4])
        wait_rows(recv_val.at[it], 496, send_sem.at[at + 5])
        wait_rows(recv_tot.at[it], TRKS - 1, send_sem.at[at + 6])


def shards(*args):
    args = args[:3] + (jnp.transpose(args[3], (1, 0, 2)),) + args[4:]
    vmem = pl.BlockSpec(memory_space=pltpu.VMEM)
    hbm = pl.BlockSpec(memory_space=pl.ANY)
    out = jax.ShapeDtypeStruct((8, KB), F32)
    vec = pltpu.VMEM((4, KB), F32)
    both = pl.pallas_call(
        kernel,
        out_shape=out,
        in_specs=[hbm] * 12,
        out_specs=vmem,
        scratch_shapes=[
            pltpu.VMEM((TILES, KB, TQ), BF16),
            pltpu.VMEM((TILES, TQ, KB), BF16),
            pltpu.VMEM((PAIRS, KB, KB), BF16),
            vec,
            vec,
            vec,
            pltpu.VMEM((9, 16, 128), F32),
            pltpu.SMEM((TILES,), I32),
            pltpu.SMEM((TILES,), I32),
            pltpu.SMEM((TILES,), I32),
            pltpu.SMEM((1,), I32),
            pltpu.SMEM((PAIRS,), I32),
            pltpu.SMEM((PAIRS,), I32),
            pltpu.VMEM((32, KB), F32),
            pltpu.VMEM((128, 128), F32),
            pltpu.VMEM((2, 32, 128), BF16),
            pltpu.VMEM((2, 1024, 128), BF16),
            pltpu.VMEM((2, 32, 128), BF16),
            pltpu.VMEM((2, 1024, 128), BF16),
            pltpu.VMEM((2, 512, 128), BF16),
            pltpu.VMEM((2, 512, 128), BF16),
            pltpu.VMEM((2, 512, 128), BF16),
            pltpu.VMEM((2, 512, 128), BF16),
            pltpu.VMEM((2, 32, 128), F32),
            pltpu.VMEM((2, TRKS, 32, 128), F32),
            pltpu.VMEM((512, 128), BF16),
            pltpu.VMEM((128, 512), BF16),
            pltpu.VMEM((48, 512), BF16),
            pltpu.VMEM((512, 128), BF16),
            pltpu.VMEM((48, 1024), BF16),
            pltpu.VMEM((32, 1024), BF16),
            pltpu.SemaphoreType.DMA((10,)),
            pltpu.SemaphoreType.DMA((TILES // CHUNK,)),
            pltpu.SemaphoreType.DMA,
            pltpu.SemaphoreType.DMA((14,)),
            pltpu.SemaphoreType.DMA((14,)),
        ],
        compiler_params=pltpu.CompilerParams(
            collective_id=1, has_side_effects=True, vmem_limit_bytes=56 * 2**20
        ),
        cost_estimate=pl.CostEstimate(flops=300_000_000, bytes_accessed=19_000_000, transcendentals=0),
        name="cg",
    )(*args)
    return both[:4], both[4:]


def solution(mesh):
    vec, both = P("cam", None), ("cam", "trk")
    tile, line = P(both, None, None), P(both)
    in_specs = (vec, vec, vec, tile, tile, line, line, line, line, tile, line, line)
    return jax.shard_map(shards, mesh=mesh, in_specs=in_specs, out_specs=(vec, vec), check_vma=False)
```

```python
import jax
import jax.numpy as jnp
from jax import lax
from jax.experimental import pallas as pl
from jax.experimental.pallas import tpu as pltpu
from jax.sharding import PartitionSpec as P

MESH = pl.DeviceIdType.MESH
F32, BF16, I32 = jnp.float32, jnp.bfloat16, jnp.int32
CAMS = 32
TRKS = 4
TILES = 24
PAIRS = 4
KB = 768
TQ = 384
CHUNK = 4
EARLY = 3
NN = (((1,), (0,)), ((), ()))
NT = (((1,), (1,)), ((), ()))


def iota(shape, dim):
    return lax.broadcasted_iota(I32, shape, dim)


def hot(mask):
    return jnp.where(mask, 1.0, 0.0).astype(BF16)


def dot(a, b, dims=NN):
    return lax.dot_general(a, b, dims, preferred_element_type=F32)


def total(a):
    return jnp.sum(jnp.sum(a, axis=0, keepdims=True), axis=1, keepdims=True)


def pack(dup):
    low = iota((8, 128), 0) < 4
    return jnp.concatenate(
        [jnp.where(low, dup[:, 256 * j : 256 * j + 128], dup[:, 256 * j + 128 : 256 * j + 256]) for j in range(3)],
        axis=0,
    )


def unpack(packed):
    low = iota((8, 128), 0) < 4
    parts = []
    for j in range(3):
        here = packed[8 * j : 8 * j + 8]
        turned = pltpu.roll(here, 4, 0)
        parts += [jnp.where(low, here, turned), jnp.where(low, turned, here)]
    return jnp.concatenate(parts, axis=1)


def triple(row):
    high = row.astype(BF16).astype(F32)
    rest = row - high
    mid = rest.astype(BF16).astype(F32)
    low = rest - mid
    sub = iota((8, 128), 0)
    return jnp.where(sub == 0, high, jnp.where(sub == 1, mid, jnp.where(sub == 2, low, 0.0)))


def kernel(
    grad_hbm, diag_hbm, prec_hbm, inv_hbm, tiles_hbm, blk_hbm, own_hbm, trk_hbm, live_hbm, covis_hbm, prow_hbm, pcol_hbm,
    both_ref,
    tiles, flipped, covis, grad_ref, diag_ref, prec_ref, inv_ref, blk_ref, own_ref, trk_ref, live_ref, prow_ref, pcol_ref,
    wide, stack, send_vec, recv_vec, send_mir, recv_mir, send_sum, recv_sum, send_val, recv_val,
    send_tot, recv_tot, to_slots, from_slots, gather_rows, scatter_rows, pick_cols, add_mir,
    vec_now, residual_now, image_now, total_now, inners_first, points_now,
    load_sem, tile_sem, covis_sem, send_sem, recv_sem,
):
    me, trk = lax.axis_index("cam"), lax.axis_index("trk")
    core, chip = me % 2, me // 2

    small = [
        pltpu.make_async_copy(src, dst, load_sem.at[i])
        for i, (src, dst) in enumerate(
            (
                (own_hbm, own_ref),
                (trk_hbm, trk_ref),
                (blk_hbm, blk_ref),
                (live_hbm, live_ref),
                (prow_hbm, prow_ref),
                (pcol_hbm, pcol_ref),
                (grad_hbm, grad_ref),
                (diag_hbm, diag_ref),
                (prec_hbm, prec_ref),
                (inv_hbm, inv_ref),
            )
        )
    ]
    for copy in small[:-1]:
        copy.start()

    def load_chunk(c):
        part = pl.ds(c * CHUNK, CHUNK)
        return pltpu.make_async_copy(tiles_hbm.at[part], tiles.at[part], tile_sem.at[c])

    load_pairs = pltpu.make_async_copy(covis_hbm, covis, covis_sem)

    barrier = pltpu.get_barrier_semaphore()

    def far_first(j):
        m = 31 - j
        return m ^ ((m >> 1) & 10)

    def greet(j, carry):
        pl.semaphore_signal(barrier, inc=1, device_id=(me ^ far_first(j), trk), device_id_type=MESH)
        return carry

    lax.fori_loop(0, CAMS - 1, greet, 0)
    for j in range(1, TRKS):
        pl.semaphore_signal(barrier, inc=1, device_id=(me, trk ^ j), device_id_type=MESH)
    for c in range(TILES // CHUNK):
        load_chunk(c).start()
    small[-1].start()
    load_pairs.start()

    def remote(src, dst, sem, to):
        pltpu.make_async_remote_copy(
            src, dst, send_sem.at[sem], recv_sem.at[sem], device_id=to, device_id_type=MESH
        ).start()

    def wait_rows(ref, rows, sem):
        part = ref.at[pl.ds(0, rows)]
        pltpu.make_async_copy(part, part, sem).wait()

    def exchange_all(src, dst, sem):
        def step(j, carry):
            peer = me ^ far_first(j)
            part = src.at[pl.ds(pl.multiple_of(peer * 16, 16), 16)]
            remote(part, dst.at[pl.ds(pl.multiple_of(me * 16, 16), 16)], sem, (peer, trk))
            return carry

        lax.fori_loop(0, CAMS - 1, step, 0)

    mine = pl.ds(pl.multiple_of(me * 16, 16), 16)
    place = pl.ds(pl.multiple_of(core * 512 + chip * 32, 32), 32)
    half = pl.ds(pl.multiple_of(core * 512, 512), 512)

    def gather_start(message, src, dst, sem):
        src[...] = message
        dst[place, :] = message

        def step(j, carry):
            m = 15 - j
            m = m ^ ((m >> 1) & 5)
            remote(src, dst.at[place], sem, (me ^ (2 * m), trk))
            return carry

        lax.fori_loop(0, CAMS // 2 - 1, step, 0)

    def gather_relay(dst, sem):
        wait_rows(dst, 480, recv_sem.at[sem])
        remote(dst.at[half], dst.at[half], sem + 1, (me ^ 1, trk))

    def gather_end(dst, sem):
        wait_rows(dst, 512, recv_sem.at[sem + 1])

    for copy in small[:-1]:
        copy.wait()

    def doubled(ref):
        value = ref[...]
        return jnp.concatenate([value, value], axis=0)

    grad, diag, prec = doubled(grad_ref), doubled(diag_ref), doubled(prec_ref)
    first = prec * grad

    lane = iota((1, 128), 1)
    lane32 = lane & 31
    eye = iota((128, 128), 0) == iota((128, 128), 1)

    def to_col(row):
        return jnp.sum(jnp.where(eye, row, 0.0), axis=1, keepdims=True)

    owner = jnp.full((1, 128), -1, I32)
    track = jnp.zeros((1, 128), I32)
    block = jnp.full((1, 128), -1, I32)
    for i in range(TILES):
        here = lane32 == i
        owner = jnp.where(here, own_ref[i], owner)
        track = jnp.where(here, trk_ref[i], track)
        block = jnp.where(here, blk_ref[i], block)
    owner = jnp.where(lane32 < live_ref[0], owner, -1).astype(F32)
    owner_col = to_col(owner)
    track_col = to_col(track.astype(F32))
    block_col = to_col(block.astype(F32))
    earlier = (owner_col[:32] == owner) & (iota((32, 128), 0) < lane32) & (owner >= 0.0)
    rank = jnp.sum(jnp.where(earlier, 1.0, 0.0), axis=0, keepdims=True)
    rank_col = to_col(rank)
    slot = jnp.where(
        (owner >= 0.0) & (lane < 96), owner * 16.0 + (lane >> 5).astype(F32) * 4.0 + rank, -1.0
    )
    slot_col = to_col(slot)
    slot_of = jnp.where(owner_col >= 0.0, owner_col * 4.0 + rank_col, -1.0)[:32]
    table = jnp.sum(
        jnp.where(slot_of == iota((32, 128), 1).astype(F32), track_col[:32] + 1.0, 0.0), axis=0, keepdims=True
    )
    pair_cols = jnp.zeros((1, 128), I32)
    for k in range(PAIRS):
        pair_cols = jnp.where((lane & 3) == k, pcol_ref[k], pair_cols)
    sub8 = iota((8, 128), 0)
    routes = jnp.where(sub8 == 0, table, jnp.where(sub8 == 1, pair_cols.astype(F32), 0.0))

    def with_rows(packed, extra):
        return jnp.concatenate([packed, extra], axis=0)

    pl.semaphore_wait(barrier, CAMS - 1 + TRKS - 1)

    gather_start(with_rows(pack(first), routes).astype(BF16), send_vec.at[0], recv_vec.at[0], 0)

    to_slots[...] = hot(iota((512, 128), 0).astype(F32) == slot)
    extra_rows = iota((128, 512), 0) - 96
    from_slots[...] = hot(
        (iota((128, 512), 1).astype(F32) == slot_col)
        | ((extra_rows >= 0) & (extra_rows < 3) & ((iota((128, 512), 1) & 15) == 12 + extra_rows))
    )
    row48 = iota((48, 1), 0)
    base = jnp.zeros((48, 1), I32)
    for k in range(PAIRS):
        cam = pcol_ref[k] // 4
        base = jnp.where((row48 & 3) == k, (cam % 2) * 512 + (cam // 2) * 32 + pcol_ref[k] % 4, base)
    base = base + (row48 >> 3) * 4
    pick_cols[...] = hot(iota((48, 1024), 1) == base)
    stack[...] = jnp.zeros((128, 128), F32)
    rows8 = iota((8, 1), 0)
    prow_col = jnp.zeros((8, 1), I32)
    for k in range(PAIRS):
        prow_col = jnp.where((rows8 & 3) == k, prow_ref[k], prow_col)
    rows_wide = iota((8, KB), 0)
    rows_tq = iota((8, TQ), 0)

    def unstack(rows, at, count):
        return jnp.concatenate([rows[at * j : at * j + 8] for j in range(count)], axis=1)

    def forward(vec, load):
        picked = jnp.zeros((32, KB), F32)
        for b in range(4):
            picked = jnp.where(block_col[:32] == b, vec[b : b + 1], picked)
        wide[...] = picked

        def group(g, carry):
            here = wide[pl.ds(pl.multiple_of(g * 8, 8), 8), :]
            out = jnp.zeros((8, TQ), F32)
            for r in range(8):
                if load and r % CHUNK == 0:
                    load_chunk(g * (8 // CHUNK) + r // CHUNK).wait()
                out = out + dot(jnp.where(rows_wide == r, here, 0.0).astype(BF16), tiles[g * 8 + r])
                if load and r % CHUNK < EARLY:
                    flip(g * 8 + r)
            for j in range(3):
                stack[pl.ds(pl.multiple_of(j * 32 + g * 8, 8), 8), :] = out[:, 128 * j : 128 * j + 128]
            return carry

        lax.fori_loop(0, TILES // 8, group, 0)

    def send_sums(src, dst, sem):
        src[...] = dot(to_slots[...], stack[...].astype(BF16)).astype(BF16)
        dst[mine, :] = src[mine, :]
        exchange_all(src, dst, sem)

    def flip(i):
        flipped[i] = tiles[i].T

    late = CHUNK - EARLY

    def flip_late(k, carry):
        flip((k // late) * CHUNK + EARLY + k % late)
        return carry

    def couple(vec):
        rows = jnp.zeros((8, KB), F32)
        for b in range(4):
            rows = jnp.where(prow_col == b, vec[b : b + 1], rows)
        mirrored = jnp.zeros((8, KB), F32)
        for k in range(PAIRS):
            mirrored = mirrored + dot(jnp.where((rows_wide & 3) == k, rows, 0.0).astype(BF16), covis[k])
        return mirrored

    def couple_rows(cols):
        out = jnp.zeros((8, KB), F32)
        for k in range(PAIRS):
            lhs = jnp.where((rows_wide & 3) == prow_ref[k], cols[k : k + 1], 0.0).astype(BF16)
            out = out + dot(lhs, covis[k], NT)
        return out

    def backward(values, start):
        points_now[...] = values

        def group(g, out):
            here = jnp.concatenate(
                [points_now[pl.ds(pl.multiple_of(32 * j + 8 * g, 8), 8), :] for j in range(3)], axis=1
            )
            for r in range(8):
                lhs = jnp.where((rows_tq & 3) == blk_ref[g * 8 + r], here[r : r + 1], 0.0).astype(BF16)
                out = out - dot(lhs, flipped[g * 8 + r])
            return out

        return lax.fori_loop(0, TILES // 8, group, start)

    def points(sums):
        parts = []
        for a in range(3):
            part = jnp.zeros((16, 128), F32)
            for e in range(3):
                part = part + inv_ref[3 * a + e] * sums[16 * e : 16 * e + 16]
            parts.append(part)
        return jnp.concatenate(parts, axis=0)

    def owners(sums_recv, src, dst, sem, own_quad):
        sums = dot(gather_rows[...], sums_recv[...])
        values = points(sums)
        inner = triple(own_quad - jnp.sum(sums * values, axis=0, keepdims=True))
        fill = jnp.concatenate([values, inner, jnp.zeros((72, 128), F32)], axis=0).astype(BF16)
        src[...] = dot(scatter_rows[...], fill).astype(BF16)
        dst[mine, :] = src[mine, :]
        exchange_all(src, dst, sem)

    def quad_row(wide_rows):
        rows = sum(wide_rows[:, 128 * j : 128 * j + 128] for j in range(6))
        return jnp.sum(rows, axis=0, keepdims=True)

    def scalars(*values):
        row = jnp.zeros((1, 128), F32)
        for k, value in enumerate(values):
            row = jnp.where(lane == k, value, row)
        return triple(row)

    def sum_trk(local, mir, values, src, dst, sem):
        quads = values[96:97] + values[97:98] + values[98:99]
        quads = jnp.where(lane == 0, jnp.sum(quads, axis=1, keepdims=True), 0.0)
        inners = mir[24:25] + mir[25:26] + mir[26:27] + quads
        src[...] = with_rows(pack(local) + mir[:24], jnp.where(sub8 == 0, inners, 0.0))
        for j in (2, 1, 3):
            remote(src, dst.at[trk], sem, (me, trk ^ j))
        dst[trk] = src[...]
        wait_rows(dst, TRKS - 1, recv_sem.at[sem])
        return (dst[0] + dst[1]) + (dst[2] + dst[3])

    def make_tables():
        got = recv_vec[0]
        select = iota((64, 1), 0)
        source = jnp.where(select < 32, (select & 1) * 512 + (select >> 1) * 32 + 24, (select & 31) * 32 + 25)
        tables = dot(hot(iota((64, 1024), 1) == source), got)
        mine4 = dot(tables[:32].astype(BF16), hot(iota((128, 128), 0) == me * 4 + (iota((128, 128), 1) & 3)))
        row_codes, col_codes = [], []
        sub32, lane32x = iota((32, 128), 0), iota((32, 128), 1)
        chunk = (lane >> 2) & 3
        for q in range(4):
            value = jnp.sum(jnp.where(sub32 == 8 * q + (lane32x >> 4), mine4, 0.0), axis=0, keepdims=True)
            code = jnp.where((value > 0.0) & (chunk < 3), chunk.astype(F32) * 16.0 + value - 1.0, -1.0)
            row_codes.append(code)
            code = jnp.where((chunk == 3) & ((lane & 3) < 3), 48.0 + (lane & 3).astype(F32), code)
            col_codes.append(to_col(code))
        gather_rows[...] = hot(iota((48, 512), 0).astype(F32) == jnp.concatenate(row_codes, axis=1))
        scatter_rows[...] = hot(iota((512, 128), 1).astype(F32) == jnp.concatenate(col_codes, axis=0))
        mir_codes = []
        part = (lane >> 2) & 7
        for q in range(8):
            value = jnp.sum(jnp.where(sub32 == 4 * q + (lane32x >> 5), tables[32:], 0.0), axis=0, keepdims=True)
            local = value - (me * 4).astype(F32)
            code = jnp.where((local >= 0.0) & (local < 4.0), part.astype(F32) * 4.0 + local, -1.0)
            mir_codes.append(jnp.where(part < 6, code, (lane & 31).astype(F32)))
        add_mir[...] = hot(iota((32, 1024), 0).astype(F32) == jnp.concatenate(mir_codes, axis=1))


    def application(it, carry):
        at = 7 * it
        vec = vec_now[...]
        pl.when(it == 0)(lambda: forward(vec, True))
        pl.when(it == 1)(lambda: forward(vec, False))
        send_sums(send_sum.at[it], recv_sum.at[it], at + 2)

        gather_relay(recv_vec.at[it], at)

        @pl.when(it == 0)
        def _():
            small[-1].wait()
            load_pairs.wait()

        mirrored = couple(vec)
        inner = scalars(0.0, 0.125 * total(residual_now[...] * vec), 0.125 * total(vec * image_now[...]))
        gather_start(with_rows(pack(mirrored), inner).astype(BF16), send_mir.at[it], recv_mir.at[it], at + 3)
        gather_end(recv_vec.at[it], at)
        pl.when(it == 0)(make_tables)
        cols = unstack(dot(pick_cols[...], recv_vec[it]), 8, 6)
        own_quad = quad_row(cols * mirrored + 0.125 * vec * diag * vec)

        @pl.when(it == 0)
        def _():
            lax.fori_loop(0, 3, flip_late, 0)

        wait_rows(recv_sum.at[it], 496, recv_sem.at[at + 2])
        owners(recv_sum.at[it], send_val.at[it], recv_val.at[it], at + 5, own_quad)
        gather_relay(recv_mir.at[it], at + 3)
        coupled = couple_rows(cols)

        @pl.when(it == 0)
        def _():
            lax.fori_loop(3, TILES // CHUNK * late, flip_late, 0)

        gather_end(recv_mir.at[it], at + 3)
        mir = dot(add_mir[...], recv_mir[it])
        wait_rows(recv_val.at[it], 496, recv_sem.at[at + 5])
        values = dot(from_slots[...], recv_val[it])
        local = backward(values, coupled)
        summed = sum_trk(local, mir, values, send_tot.at[it], recv_tot.at[it], at + 6)

        @pl.when(it == 0)
        def _():
            image = diag * vec + unpack(summed[:24])
            residual = grad - (summed[24:25, 1:2] / summed[24:25, 0:1]) * image
            after = prec * residual
            gather_start(
                with_rows(pack(after), jnp.zeros((8, 128), F32)).astype(BF16), send_vec.at[1], recv_vec.at[1], 7
            )
            vec_now[...] = after
            image_now[...] = image
            residual_now[...] = residual
            inners_first[...] = summed[24:32]

        @pl.when(it == 1)
        def _():
            total_now[...] = summed

        return carry

    vec_now[...] = first
    residual_now[...] = grad
    image_now[...] = jnp.zeros((8, KB), F32)
    lax.fori_loop(0, 2, application, 0)

    vec, image, residual, summed = vec_now[...], image_now[...], residual_now[...], total_now[...]
    dim, rz = inners_first[0:1, 0:1], inners_first[0:1, 1:2]
    alpha = rz / dim
    inners = summed[24:25]
    fresh, cross = inners[:, 1:2], inners[:, 2:3]
    beta = fresh / rz
    second = diag * vec + unpack(summed[:24]) + beta * image
    curve = inners[:, 0:1] + beta * (2.0 * cross + beta * dim)
    alpha_next = fresh / curve
    step = alpha * first + alpha_next * (vec + beta * first)
    both_ref[...] = jnp.where(iota((8, KB), 0) < 4, step, residual - alpha_next * second)

    for it in range(2):
        at = 7 * it
        wait_rows(recv_vec.at[it], 480, send_sem.at[at])
        wait_rows(recv_vec.at[it], 512, send_sem.at[at + 1])
        wait_rows(recv_sum.at[it], 496, send_sem.at[at + 2])
        wait_rows(recv_mir.at[it], 480, send_sem.at[at + 3])
        wait_rows(recv_mir.at[it], 512, send_sem.at[at + 4])
        wait_rows(recv_val.at[it], 496, send_sem.at[at + 5])
        wait_rows(recv_tot.at[it], TRKS - 1, send_sem.at[at + 6])


def shards(*args):
    args = args[:3] + (jnp.transpose(args[3], (1, 0, 2)),) + args[4:]
    vmem = pl.BlockSpec(memory_space=pltpu.VMEM)
    hbm = pl.BlockSpec(memory_space=pl.ANY)
    out = jax.ShapeDtypeStruct((8, KB), F32)
    vec = pltpu.VMEM((4, KB), F32)
    both = pl.pallas_call(
        kernel,
        out_shape=out,
        in_specs=[hbm] * 12,
        out_specs=vmem,
        scratch_shapes=[
            pltpu.VMEM((TILES, KB, TQ), BF16),
            pltpu.VMEM((TILES, TQ, KB), BF16),
            pltpu.VMEM((PAIRS, KB, KB), BF16),
            vec,
            vec,
            vec,
            pltpu.VMEM((9, 16, 128), F32),
            pltpu.SMEM((TILES,), I32),
            pltpu.SMEM((TILES,), I32),
            pltpu.SMEM((TILES,), I32),
            pltpu.SMEM((1,), I32),
            pltpu.SMEM((PAIRS,), I32),
            pltpu.SMEM((PAIRS,), I32),
            pltpu.VMEM((32, KB), F32),
            pltpu.VMEM((128, 128), F32),
            pltpu.VMEM((2, 32, 128), BF16),
            pltpu.VMEM((2, 1024, 128), BF16),
            pltpu.VMEM((2, 32, 128), BF16),
            pltpu.VMEM((2, 1024, 128), BF16),
            pltpu.VMEM((2, 512, 128), BF16),
            pltpu.VMEM((2, 512, 128), BF16),
            pltpu.VMEM((2, 512, 128), BF16),
            pltpu.VMEM((2, 512, 128), BF16),
            pltpu.VMEM((2, 32, 128), F32),
            pltpu.VMEM((2, TRKS, 32, 128), F32),
            pltpu.VMEM((512, 128), BF16),
            pltpu.VMEM((128, 512), BF16),
            pltpu.VMEM((48, 512), BF16),
            pltpu.VMEM((512, 128), BF16),
            pltpu.VMEM((48, 1024), BF16),
            pltpu.VMEM((32, 1024), BF16),
            pltpu.VMEM((8, KB), F32),
            pltpu.VMEM((8, KB), F32),
            pltpu.VMEM((8, KB), F32),
            pltpu.VMEM((32, 128), F32),
            pltpu.VMEM((8, 128), F32),
            pltpu.VMEM((128, 128), F32),
            pltpu.SemaphoreType.DMA((10,)),
            pltpu.SemaphoreType.DMA((TILES // CHUNK,)),
            pltpu.SemaphoreType.DMA,
            pltpu.SemaphoreType.DMA((14,)),
            pltpu.SemaphoreType.DMA((14,)),
        ],
        compiler_params=pltpu.CompilerParams(
            collective_id=1, has_side_effects=True, vmem_limit_bytes=56 * 2**20
        ),
        cost_estimate=pl.CostEstimate(flops=300_000_000, bytes_accessed=19_000_000, transcendentals=0),
        name="cg",
    )(*args)
    return both[:4], both[4:]


def solution(mesh):
    vec, both = P("cam", None), ("cam", "trk")
    tile, line = P(both, None, None), P(both)
    in_specs = (vec, vec, vec, tile, tile, line, line, line, line, tile, line, line)
    return jax.shard_map(shards, mesh=mesh, in_specs=in_specs, out_specs=(vec, vec), check_vma=False)
```
